128 devices in a mesh: row: 8 (over y_lo, z), col: 16 (over y_hi, x, core).
Axes of the slice: x: 4, y: 4 (y_hi: 2, y_lo: 2; y = y_hi * 2 + y_lo), z: 4, core: 2. Of those that a mesh axis runs over, the one named last changes fastest.
Arguments:
- images: bfloat16 [65536, 2, 4096], P(('row', 'col')), may hold values from -320 to 320
- precision: float32 [65536], P(('row', 'col')), may hold values from 0.001 to 0.01
- templates: bfloat16 [128, 2, 4096], P(('row', 'col')), may hold values from -4 to 4
- template_id: int32 [128], replicated, may hold values from 0 to 127, as said below
- shift_table: int32 [128, 8], replicated, may hold values from 0 to 63, as said below
Outputs:
- updated: float32 [128, 2, 4096], P(('row', 'col'))
The draws below stay inside these ranges and needn't reach their ends.
Inputs may be any that keep to these rules, and one draw needn't show every extreme that they name: `template_id`: A permutation of 0 to 127. `shift_table`: each row holds 8 different shift numbers.
All inputs are finite; a program needn't handle non-finite values.
Results may differ from the reference program's by a relative error of at most 0.00058.
Values may be sent and summed in bfloat16 or wider, within the bound.
A program may use at most 192 MiB of HBM per device.

```python
import math
import jax
import jax.numpy as jnp
from jax import lax

GRID = 64
HALF = 4096
K = 128
SH = 8
NSHIFT = 64
IMG_DEV = 512
IMAGES = 65536


def phase_tables_drawn(grid_side):
    coefficient = jnp.arange(grid_side * grid_side, dtype=jnp.int32)
    freq_x = coefficient // grid_side - grid_side // 2
    freq_y = coefficient % grid_side - grid_side // 2
    shift_number = jnp.arange(64, dtype=jnp.int32)
    step_x = shift_number // 8 - 4
    step_y = shift_number % 8 - 4
    phase_index = (step_x[:, None] * freq_x[None, :] + step_y[:, None] * freq_y[None, :]) % grid_side
    angle_value = phase_index.astype(jnp.float32) * (2.0 * math.pi / grid_side)
    return (jnp.cos(angle_value), jnp.sin(angle_value))


def shared_truth(key):
    base = jax.random.fold_in(key, 101)
    key_maps, key_order, key_shift = jax.random.split(base, 3)
    noise = jnp.clip(jax.random.normal(key_maps, (K, 2, HALF), jnp.float32), -5.0, 5.0)
    rough = jnp.exp(jax.random.uniform(jax.random.fold_in(key_maps, 3), (K, 2, HALF), jnp.float32, -0.7, 0.7))
    true_maps = noise * rough
    template_ids = jax.random.permutation(key_order, K).astype(jnp.int32)
    ranking = jax.random.randint(key_shift, (K, NSHIFT), 0, 1 << 20) * NSHIFT + jnp.arange(NSHIFT, dtype=jnp.int32)[None, :]
    shift_rows = jnp.argsort(ranking, axis=1)[:, :SH].astype(jnp.int32)
    return (true_maps, template_ids, shift_rows)


def draw_template_id(key, part):
    return shared_truth(key)[1]


def draw_shift_table(key, part):
    return shared_truth(key)[2]


def draw_templates(key, part):
    true_maps, template_ids, shift_rows = shared_truth(key)
    noise_key = jax.random.fold_in(key, 202)
    jitter = 0.15 * jnp.clip(jax.random.normal(noise_key, (K, 2, HALF), jnp.float32), -5.0, 5.0)
    return (0.3 * true_maps[template_ids] + jitter).astype(jnp.bfloat16)


def draw_images(key, part):
    true_maps, template_ids, shift_rows = shared_truth(key)
    cos_table, sin_table = phase_tables_drawn(GRID)

    def make_block(block_index):
        block_key = jax.random.fold_in(jax.random.fold_in(key, 303), block_index)
        key_pick, key_slot, key_noise = jax.random.split(block_key, 3)
        picked = jax.random.randint(key_pick, (IMG_DEV,), 0, K)
        slot_index = jax.random.randint(key_slot, (IMG_DEV,), 0, SH)
        shift_number = shift_rows[picked, slot_index]
        maps = true_maps[picked]
        cosine = cos_table[shift_number]
        sine_table = sin_table[shift_number]
        real_part = maps[:, 0] * cosine + maps[:, 1] * sine_table
        imag_part = maps[:, 1] * cosine - maps[:, 0] * sine_table
        signal = 0.3 * jnp.stack([real_part, imag_part], axis=1)
        noise = jnp.clip(jax.random.normal(key_noise, (IMG_DEV, 2, HALF), jnp.float32), -5.0, 5.0)
        return (signal + noise).astype(jnp.bfloat16)
    blocks = lax.map(make_block, jnp.arange(IMAGES // IMG_DEV, dtype=jnp.int32))
    return blocks.reshape(IMAGES, 2, HALF)


def levels(key, shape, pieces, low, top_value):
    def one(axis_at, parts):
        draws = jax.random.uniform(jax.random.fold_in(jax.random.fold_in(key, 6), axis_at), (parts,), jnp.float32, low / len(pieces), top_value / len(pieces))
        return jnp.repeat(jnp.exp(draws), shape[axis_at] // parts).reshape((-1,) + (1,) * (len(shape) - axis_at - 1))

    loudness = one(*pieces[0])
    for cut in pieces[1:]:
        loudness = loudness * one(*cut)
    return loudness


def setup_inputs(seed: int = 0) -> dict:
    splits = jax.random.split(jax.random.key(seed), 6)
    images = draw_images(jax.random.fold_in(splits[5], 71), 0)
    precision = jnp.clip(jnp.exp(math.log(0.01) - 2.30258502 * jax.random.uniform(splits[1], (IMAGES,), jnp.float32) ** levels(splits[1], (IMAGES,), ((0, 128),), -0.2, 0.2)), 0.001, 0.01)
    templates = draw_templates(jax.random.fold_in(splits[5], 71), 0)
    template_id = draw_template_id(jax.random.fold_in(splits[5], 71), 0)
    shift_table = draw_shift_table(jax.random.fold_in(splits[5], 71), 0)
    return dict(images=images, precision=precision, templates=templates, template_id=template_id, shift_table=shift_table)


PRIOR_WEIGHT = 4.0


def phase_tables(grid_side):
    coefficient = jnp.arange(grid_side * grid_side, dtype=jnp.int32)
    freq_x = coefficient // grid_side - grid_side // 2
    freq_y = coefficient % grid_side - grid_side // 2
    shift_number = jnp.arange(64, dtype=jnp.int32)
    step_x = shift_number // 8 - 4
    step_y = shift_number % 8 - 4
    phase_index = (step_x[:, None] * freq_x[None, :] + step_y[:, None] * freq_y[None, :]) % grid_side
    angle_value = phase_index.astype(jnp.float32) * (2.0 * math.pi / grid_side)
    return jnp.cos(angle_value), jnp.sin(angle_value)


def shift_forward(real_part, imag_part, cosine, sine_table):
    return real_part * cosine + imag_part * sine_table, imag_part * cosine - real_part * sine_table


def shift_back(real_part, imag_part, cosine, sine_table):
    return real_part * cosine - imag_part * sine_table, imag_part * cosine + real_part * sine_table


def reference(images, precision, templates, template_id, shift_table):
    cos_table, sin_table = phase_tables(GRID)
    template_f = templates.astype(jnp.float32)
    shift_rows = shift_table[template_id]
    cosine = cos_table[shift_rows]
    sine_table = sin_table[shift_rows]
    real_part, imag_part = shift_forward(template_f[:, None, 0], template_f[:, None, 1], cosine, sine_table)
    rotated = jnp.stack([real_part, imag_part], axis=2).astype(jnp.bfloat16).reshape(K * SH, 2 * HALF)
    half_norm = jnp.repeat(0.5 * jnp.sum(template_f * template_f, axis=(1, 2)), SH)
    image_blocks = images.reshape(IMAGES // IMG_DEV, IMG_DEV, 2 * HALF)
    precision_blocks = precision.reshape(IMAGES // IMG_DEV, IMG_DEV)

    def scan_step(state_pair, block_pair):
        numerator, denominator = state_pair
        image_rows, block_precision = block_pair
        inner_products = jnp.dot(image_rows, rotated.T, preferred_element_type=jnp.float32)
        scores = block_precision[:, None] * (inner_products - half_norm[None, :])
        highest = jnp.max(scores, axis=1, keepdims=True)
        exponent = jnp.exp(scores - highest)
        weights = (exponent / jnp.sum(exponent, axis=1, keepdims=True)).astype(jnp.bfloat16)
        numerator = numerator + jnp.dot(weights.T, image_rows, preferred_element_type=jnp.float32)
        denominator = denominator + jnp.sum(weights.astype(jnp.float32), axis=0)
        return (numerator, denominator), None

    initial = (jnp.zeros((K * SH, 2 * HALF), jnp.float32), jnp.zeros((K * SH,), jnp.float32))
    (numerator, denominator), _ = lax.scan(scan_step, initial, (image_blocks, precision_blocks))
    numerator = numerator.reshape(K, SH, 2, HALF)
    back_real, back_imag = shift_back(numerator[:, :, 0], numerator[:, :, 1], cosine, sine_table)
    summed = jnp.stack([jnp.sum(back_real, axis=1), jnp.sum(back_imag, axis=1)], axis=1)
    totals = jnp.sum(denominator.reshape(K, SH), axis=1)
    return (summed + PRIOR_WEIGHT * template_f) / (totals + PRIOR_WEIGHT)[:, None, None]
```

```python
import functools

import jax
import jax.numpy as jnp
import ml_dtypes
import numpy as np
from jax import lax
from jax.experimental import pallas as pl
from jax.experimental.pallas import tpu as pltpu
from jax.sharding import PartitionSpec as P

MESH = pl.DeviceIdType.MESH
F32 = jnp.float32
BF16 = jnp.bfloat16

GRID = 64
COEFFS = 4096
TEMPLATES = 128
SHIFTS = 8
PAIRS = TEMPLATES * SHIFTS
N_IMG = 512
ROWS = 64
ROWS_ALL = 72
STEP = 512
STEPS = 2 * COEFFS // STEP
PRIOR_WEIGHT = 4.0
MIB = 1 << 20

ORDERS = ((2, 1, 0), (1, 0, 2), (0, 2, 1))


def phase_constant():
    c = np.arange(COEFFS)
    fx = c // GRID - GRID // 2
    fy = c % GRID - GRID // 2
    s = np.arange(64)
    k = ((s // 8 - 4)[:, None] * fx[None] + (s % 8 - 4)[:, None] * fy[None]) % GRID
    angle = k * (2.0 * np.pi / GRID)
    both = np.stack([np.cos(angle), np.sin(angle)], 1).reshape(64, 2, 32, 128)
    both = both.transpose(0, 2, 1, 3).reshape(64, 2 * COEFFS).astype(np.float32)
    high = both.astype(ml_dtypes.bfloat16)
    rest = both - high.astype(np.float32)
    mid = rest.astype(ml_dtypes.bfloat16)
    low = (rest - mid.astype(np.float32)).astype(ml_dtypes.bfloat16)
    return np.concatenate([high, mid, low], 0)


def place():
    row, col = lax.axis_index("row"), lax.axis_index("col")
    z, y_lo = row % 4, row // 4
    core, x, y_hi = col % 2, (col // 2) % 4, col // 8
    return core, (z, y_hi * 2 + y_lo, x)


def device(core, at):
    z, y, x = at
    return ((y % 2) * 4 + z, ((y // 2) * 4 + x) * 2 + core)


def moved(at, axis, by):
    return tuple((v + by) % 4 if i == axis else v for i, v in enumerate(at))


def enter(core, at):
    barrier = pltpu.get_barrier_semaphore()
    others = [device(1 - core, at)]
    others += [device(core, moved(at, a, d)) for a in range(3) for d in (1, 2, 3)]
    for other in others:
        pl.semaphore_signal(barrier, inc=1, device_id=other, device_id_type=MESH)
    pl.semaphore_wait(barrier, len(others))


def gather_kernel(t_ref, g_ref, send_sem, recv_sem):
    core, at = place()
    enter(core, at)
    g_ref[core, at[0], at[1], at[2]] = t_ref[...]
    groups = [(pl.ds(16 * g, 16), (ORDERS + ORDERS)[g]) for g in range(4)]

    def view(rows, order, stage, where):
        done = order[:stage]
        index = tuple(slice(None) if a in done else where[a] for a in range(3))
        return g_ref.at[(core,) + index + (rows,)]

    def copy(g, stage, d, arrived=False):
        rows, order = groups[g]
        if stage == 3:
            ref = g_ref.at[1 - core if arrived else core, :, :, :, rows]
            target = device(1 - core, at)
        else:
            axis = order[stage]
            ref = view(rows, order, stage, moved(at, axis, 4 - d) if arrived else at)
            target = device(core, moved(at, axis, d))
        return pltpu.make_async_remote_copy(
            src_ref=ref, dst_ref=ref, send_sem=send_sem.at[g, stage, d - 1],
            recv_sem=recv_sem.at[g, stage, d - 1], device_id=target, device_id_type=MESH)

    def each(stage):
        return (1, 3, 2) if stage < 3 else (1,)

    for stage in range(4):
        for g in range(4):
            if stage:
                for d in each(stage - 1):
                    copy(g, stage - 1, d, True).wait_recv()
            for d in each(stage):
                copy(g, stage, d).start()
    for g in range(4):
        copy(g, 3, 1, True).wait_recv()
    for stage in range(4):
        for g in range(4):
            for d in each(stage):
                copy(g, stage, d).wait_send()


def scatter_kernel(p_in, t_ref, out_ref, p_ref, r0, r1, r2, r3, send_sem, recv_sem, load_sem):
    core, at = place()
    load = pltpu.make_async_copy(p_in, p_ref, load_sem)
    load.start()
    enter(core, at)
    load.wait()
    lands = (r0, r1, r2, r3)

    def kept(order, stage):
        return (core,) + tuple(at[a] if a in order[:stage] else slice(None) for a in range(3))

    def copy(k, o, stage, d):
        rows = pl.ds(pl.multiple_of(k * 8, 8), 8)
        order = ORDERS[o]
        if stage == 0:
            src = p_ref.at[1 - core, :, :, :, rows]
            dst = r0.at[:, :, :, rows]
            target = device(1 - core, at)
        else:
            axis = order[stage - 1]
            other = moved(at, axis, d)
            index = [at[a] if a in order[:stage - 1] else slice(None) for a in range(3)]
            index[axis] = other[axis]
            src = p_ref.at[(core,) + tuple(index) + (rows,)]
            dst = lands[stage].at[(d - 1,) + (slice(None),) * (3 - stage) + (rows,)]
            target = device(core, other)
        return pltpu.make_async_remote_copy(
            src_ref=src, dst_ref=dst, send_sem=send_sem.at[k, stage, d - 1],
            recv_sem=recv_sem.at[k, stage, d - 1], device_id=target, device_id_type=MESH)

    def each(stage):
        return (1, 3, 2) if stage else (1,)

    def take(k, o, stage):
        rows = pl.ds(pl.multiple_of(k * 8, 8), 8)
        for d in each(stage):
            copy(k, o, stage, d).wait_recv()
        index = kept(ORDERS[o], stage) + (rows,)
        total = p_ref[index]
        if stage == 0:
            total += r0[:, :, :, rows]
        else:
            for d in (1, 2, 3):
                total += lands[stage][(d - 1,) + (slice(None),) * (3 - stage) + (rows,)]
        p_ref[index] = total

    for stage in range(4):
        @pl.loop(0, 3)
        def _(kk):
            for o in range(3):
                k = kk * 3 + o
                if stage:
                    take(k, o, stage - 1)
                for d in each(stage):
                    copy(k, o, stage, d).start()

    @pl.loop(0, 3)
    def _(kk):
        for o in range(3):
            take(kk * 3 + o, o, 3)

    @pl.loop(0, 3)
    def _(kk):
        for o in range(3):
            for stage in range(4):
                for d in each(stage):
                    copy(kk * 3 + o, o, stage, d).wait_send()

    own = p_ref[core, at[0], at[1], at[2]]
    total = jnp.sum(own[ROWS:], keepdims=True) + PRIOR_WEIGHT
    out_ref[...] = (own[:ROWS] + PRIOR_WEIGHT * t_ref[...].astype(F32)) / total


def compute_kernel(img, tab, g_ref, prec, tid, table, p_ref,
                   x, raw, wide, fac, acc, rot, wt, onehot, norm, tabs, img_sem, tab_sem):
    def fetch(b):
        return pltpu.make_async_copy(img.at[pl.ds(b * 4096, 4096)], raw.at[b % 2], img_sem.at[b % 2])

    def fetch_tab(k, slot):
        return pltpu.make_async_copy(
            tab.at[:, pl.ds(pl.multiple_of(k * STEP, STEP), STEP)], tabs.at[slot], tab_sem.at[slot])

    fetch(0).start()
    for b in range(8):
        if b < 7:
            fetch(b + 1).start()
        fetch(b).wait()
        wide[pl.ds(0, 4096)] = raw[b % 2].astype(F32)

        @pl.loop(0, ROWS)
        def _(r):
            lanes = pl.ds(pl.multiple_of(r * 128, 128), 128)
            x[pl.ds(b * 64, 64), lanes] = wide[pl.ds(r, 64, stride=ROWS), :].astype(BF16)

    ids = lax.broadcasted_iota(jnp.int32, (128, 128), 0)
    pick = jnp.where(ids == tid[...], 1.0, 0.0).astype(BF16)
    shifts_t = jnp.dot(table[...].astype(F32).astype(BF16), pick, preferred_element_type=F32)
    slot = lax.broadcasted_iota(jnp.int32, (128, 128), 1)
    row, col = slot // 16, slot % 16
    inner = (col % 2) * 64 + (row % 4) * 16 + ((col // 8) * 2 + row // 4) * 4 + (col // 2) % 4
    perm = jnp.where(ids == inner, 1.0, 0.0).astype(BF16)
    shifts = lax.dot_general(perm, shifts_t.astype(BF16), (((1,), (1,)), ((), ())),
                             preferred_element_type=F32)
    lane = lax.broadcasted_iota(jnp.int32, (128, 64), 1).astype(F32)
    for j in range(SHIFTS):
        one = jnp.where(lane == shifts[:, j:j + 1], 1.0, 0.0).astype(BF16)
        onehot[pl.ds(j * 128, 128), :] = jnp.concatenate([one, one, one], axis=1)

    @pl.loop(0, TEMPLATES)
    def _(p):
        wide[pl.ds(pl.multiple_of(p * ROWS, ROWS), ROWS)] = g_ref[p].astype(F32)

    @pl.loop(0, TEMPLATES // 8)
    def _(b):
        def add(r, total):
            t = wide[pl.ds(b * 8 * ROWS + r, 8, stride=ROWS), :]
            return total + t * t
        total = lax.fori_loop(0, ROWS, add, jnp.zeros((8, 128), F32), unroll=8)
        norm[pl.ds(pl.multiple_of(b * 8, 8), 8), :] = jnp.broadcast_to(
            0.5 * jnp.sum(total, axis=1, keepdims=True), (8, 128))

    acc[...] = jnp.zeros_like(acc)

    def factors(k):
        fetch_tab(k, 0).start()
        fetch_tab(k, 0).wait()
        fac[...] = jnp.dot(onehot[...], tabs[0], preferred_element_type=F32)

    @pl.loop(0, STEPS)
    def _(k):
        lanes = pl.ds(pl.multiple_of(k * STEP, STEP), STEP)
        factors(k)

        @pl.loop(0, TEMPLATES // 16)
        def _(b):
            for tile in range(2):
                r = 4 * k + 2 * tile
                re = wide[pl.ds(b * 16 * ROWS + r, 16, stride=ROWS), :]
                im = wide[pl.ds(b * 16 * ROWS + r + 1, 16, stride=ROWS), :]
                for j in range(SHIFTS):
                    rows = pl.ds(pl.multiple_of(j * 128 + b * 16, 16), 16)
                    c = fac[rows, tile * 256:tile * 256 + 128]
                    s = fac[rows, tile * 256 + 128:tile * 256 + 256]
                    rot[rows, tile * 256:tile * 256 + 128] = (re * c + im * s).astype(BF16)
                    rot[rows, tile * 256 + 128:tile * 256 + 256] = (im * c - re * s).astype(BF16)

        acc[...] += lax.dot_general(rot[...], x[:, lanes], (((1,), (1,)), ((), ())),
                                    preferred_element_type=F32)

    precision = prec[...]

    def score(i, top):
        rows = pl.ds(pl.multiple_of(i * 8, 8), 8)
        half = norm[pl.ds(pl.multiple_of((i % 16) * 8, 8), 8), :]
        value = precision * (acc[rows, :] - jnp.concatenate([half] * 4, axis=1))
        acc[rows, :] = value
        return jnp.maximum(top, value)

    top = lax.fori_loop(0, PAIRS // 8, score, jnp.full((8, N_IMG), -jnp.inf, F32), unroll=4)
    top = jnp.max(top, axis=0, keepdims=True)

    def exponent(i, total):
        rows = pl.ds(pl.multiple_of(i * 8, 8), 8)
        value = jnp.exp(acc[rows, :] - top)
        acc[rows, :] = value
        return total + value

    total = lax.fori_loop(0, PAIRS // 8, exponent, jnp.zeros((8, N_IMG), F32), unroll=4)
    scale = 1.0 / jnp.sum(total, axis=0, keepdims=True)

    @pl.loop(0, TEMPLATES // 16)
    def _(b):
        total = jnp.zeros((16, 128), F32)
        for j in range(SHIFTS):
            rows = pl.ds(pl.multiple_of(j * 128 + b * 16, 16), 16)
            weight = (acc[rows, :] * scale).astype(BF16)
            wt[rows, :] = weight
            weight = weight.astype(F32)
            for lanes in range(4):
                total += weight[:, lanes * 128:lanes * 128 + 128]
        p_ref[pl.ds(b * 16 * ROWS_ALL + ROWS, 16, stride=ROWS_ALL), :] = total
        for r in range(ROWS + 1, ROWS_ALL):
            p_ref[pl.ds(b * 16 * ROWS_ALL + r, 16, stride=ROWS_ALL), :] = jnp.zeros((16, 128), F32)

    @pl.loop(0, STEPS)
    def _(k):
        lanes = pl.ds(pl.multiple_of(k * STEP, STEP), STEP)
        factors(k)
        acc[...] = jnp.dot(wt[...], x[:, lanes], preferred_element_type=F32)

        @pl.loop(0, TEMPLATES // 8)
        def _(b):
            for tile in range(2):
                back_re = jnp.zeros((8, 128), F32)
                back_im = jnp.zeros((8, 128), F32)
                for j in range(SHIFTS):
                    rows = pl.ds(pl.multiple_of(j * 128 + b * 8, 8), 8)
                    c = fac[rows, tile * 256:tile * 256 + 128]
                    s = fac[rows, tile * 256 + 128:tile * 256 + 256]
                    re = acc[rows, tile * 256:tile * 256 + 128]
                    im = acc[rows, tile * 256 + 128:tile * 256 + 256]
                    back_re += re * c - im * s
                    back_im += im * c + re * s
                r = 4 * k + 2 * tile
                p_ref[pl.ds(b * 8 * ROWS_ALL + r, 8, stride=ROWS_ALL), :] = back_re
                p_ref[pl.ds(b * 8 * ROWS_ALL + r + 1, 8, stride=ROWS_ALL), :] = back_im


def body(images, precision, templates, template_id, shift_table):
    vmem = pl.BlockSpec(memory_space=pltpu.VMEM)
    anywhere = pl.BlockSpec(memory_space=pl.ANY)
    dma = pltpu.SemaphoreType.DMA
    img = images.reshape(N_IMG, 2, 32, 128).transpose(0, 2, 1, 3).reshape(N_IMG * ROWS, 128)
    own = templates.reshape(2, 32, 128).transpose(1, 0, 2).reshape(ROWS, 128)
    tab = jnp.asarray(phase_constant())
    gathered = pl.pallas_call(
        gather_kernel,
        out_shape=jax.ShapeDtypeStruct((2, 4, 4, 4, ROWS, 128), BF16),
        in_specs=[vmem], out_specs=vmem,
        scratch_shapes=[dma((4, 4, 3)), dma((4, 4, 3))],
        compiler_params=pltpu.CompilerParams(collective_id=0, has_side_effects=True,
                                             vmem_limit_bytes=16 * MIB),
        name="gather",
    )(own)
    part = pl.pallas_call(
        compute_kernel,
        out_shape=jax.ShapeDtypeStruct((TEMPLATES * ROWS_ALL, 128), F32),
        in_specs=[anywhere, anywhere, vmem, vmem, vmem, vmem], out_specs=vmem,
        scratch_shapes=[
            pltpu.VMEM((N_IMG, 2 * COEFFS), BF16),
            pltpu.VMEM((2, 4096, 128), BF16),
            pltpu.VMEM((TEMPLATES * ROWS, 128), F32),
            pltpu.VMEM((PAIRS, STEP), F32),
            pltpu.VMEM((PAIRS, N_IMG), F32),
            pltpu.VMEM((PAIRS, STEP), BF16),
            pltpu.VMEM((PAIRS, N_IMG), BF16),
            pltpu.VMEM((PAIRS, 192), BF16),
            pltpu.VMEM((TEMPLATES, 128), F32),
            pltpu.VMEM((2, 192, STEP), BF16),
            dma((2,)), dma((2,)),
        ],
        compiler_params=pltpu.CompilerParams(vmem_limit_bytes=56 * MIB),
        name="compute",
    )(img, tab, gathered.reshape(TEMPLATES, ROWS, 128), precision.reshape(1, N_IMG),
      template_id.reshape(1, TEMPLATES), shift_table.T)
    out = pl.pallas_call(
        scatter_kernel,
        out_shape=jax.ShapeDtypeStruct((ROWS, 128), F32),
        in_specs=[anywhere, vmem], out_specs=vmem,
        scratch_shapes=[
            pltpu.VMEM((2, 4, 4, 4, ROWS_ALL, 128), F32),
            pltpu.VMEM((4, 4, 4, ROWS_ALL, 128), F32),
            pltpu.VMEM((3, 4, 4, ROWS_ALL, 128), F32),
            pltpu.VMEM((3, 4, ROWS_ALL, 128), F32),
            pltpu.VMEM((3, ROWS_ALL, 128), F32),
            dma((9, 4, 3)), dma((9, 4, 3)), dma,
        ],
        compiler_params=pltpu.CompilerParams(collective_id=1, has_side_effects=True,
                                             vmem_limit_bytes=24 * MIB),
        name="scatter",
    )(part.reshape(2, 4, 4, 4, ROWS_ALL, 128), own)
    return out.reshape(32, 2, 128).transpose(1, 0, 2).reshape(1, 2, COEFFS)


def solution(mesh):
    return jax.shard_map(
        body,
        mesh=mesh,
        in_specs=(
            P(("row", "col"), None, None),
            P(("row", "col")),
            P(("row", "col"), None, None),
            P(),
            P(),
        ),
        out_specs=P(("row", "col"), None, None),
        check_vma=False,
    )
```

```python
import functools

import jax
import jax.numpy as jnp
import ml_dtypes
import numpy as np
from jax import lax
from jax.experimental import pallas as pl
from jax.experimental.pallas import tpu as pltpu
from jax.sharding import PartitionSpec as P

MESH = pl.DeviceIdType.MESH
F32 = jnp.float32
BF16 = jnp.bfloat16

GRID = 64
COEFFS = 4096
TEMPLATES = 128
SHIFTS = 8
PAIRS = TEMPLATES * SHIFTS
N_IMG = 512
ROWS = 64
STEP = 512
STEPS = 2 * COEFFS // STEP
HALF_STEPS = STEPS // 2
CHUNKS = 9
PRIOR_WEIGHT = 4.0
RB, BB = 32, 16
MIB = 1 << 20

ORDERS = ((2, 1, 0), (1, 0, 2), (0, 2, 1))


def phase_constant():
    c = np.arange(COEFFS)
    fx = c // GRID - GRID // 2
    fy = c % GRID - GRID // 2
    s = np.arange(64)
    k = ((s // 8 - 4)[:, None] * fx[None] + (s % 8 - 4)[:, None] * fy[None]) % GRID
    angle = k * (2.0 * np.pi / GRID)
    both = np.stack([np.cos(angle), np.sin(angle)], 1).reshape(64, 2, 32, 128)
    both = both.transpose(0, 2, 1, 3).reshape(64, 2 * COEFFS)[:, :COEFFS].astype(np.float32)
    high = both.astype(ml_dtypes.bfloat16)
    rest = both - high.astype(np.float32)
    mid = rest.astype(ml_dtypes.bfloat16)
    low = (rest - mid.astype(np.float32)).astype(ml_dtypes.bfloat16)
    return np.concatenate([high, mid, low], 0)


def place():
    row, col = lax.axis_index("row"), lax.axis_index("col")
    z, y_lo = row % 4, row // 4
    core, x, y_hi = col % 2, (col // 2) % 4, col // 8
    return core, (z, y_hi * 2 + y_lo, x)


def device(core, at):
    z, y, x = at
    return ((y % 2) * 4 + z, ((y // 2) * 4 + x) * 2 + core)


def moved(at, axis, by):
    return tuple((v + by) % 4 if i == axis else v for i, v in enumerate(at))


def enter(core, at):
    barrier = pltpu.get_barrier_semaphore()
    others = [device(1 - core, at)]
    others += [device(core, moved(at, a, d)) for a in range(3) for d in (1, 2, 3)]
    for other in others:
        pl.semaphore_signal(barrier, inc=1, device_id=other, device_id_type=MESH)
    pl.semaphore_wait(barrier, len(others))


def em_kernel(img, tab, own_t, prec, tid, table, out_ref,
              x, raw, wide, fac, acc, rot_a, rot_b, buf_a, buf_b, wts, onehot, sign, norm, tabs,
              got, part, r0, mine, r1, r2, r3, final,
              img_sem, tab_sem, gs_sem, gr_sem, ss_sem, sr_sem):
    core, at = place()

    groups = [(pl.ds(16 * g, 16), (ORDERS + ORDERS)[g]) for g in range(4)]

    def view(rows, order, stage, where):
        done = order[:stage]
        index = tuple(slice(None) if a in done else where[a] for a in range(3))
        return got.at[(core,) + index + (rows,)]

    def g_copy(g, stage, d, arrived=False):
        rows, order = groups[g]
        if stage == 3:
            ref = got.at[1 - core if arrived else core, :, :, :, rows]
            target = device(1 - core, at)
        else:
            axis = order[stage]
            ref = view(rows, order, stage, moved(at, axis, 4 - d) if arrived else at)
            target = device(core, moved(at, axis, d))
        return pltpu.make_async_remote_copy(
            src_ref=ref, dst_ref=ref, send_sem=gs_sem.at[g, stage, d - 1],
            recv_sem=gr_sem.at[g, stage, d - 1], device_id=target, device_id_type=MESH)

    def g_each(stage):
        return (1, 3, 2) if stage < 3 else (1,)

    def g_stage(stage):
        for g in range(4):
            if stage:
                for d in g_each(stage - 1):
                    g_copy(g, stage - 1, d, True).wait_recv()
            if stage < 4:
                for d in g_each(stage):
                    g_copy(g, stage, d).start()

    lands = (r0, r1, r2, r3)

    def s_copy(c, o, stage, d):
        order = ORDERS[o]
        if stage == 0:
            src = part.at[pl.ds(pl.multiple_of(c * 1024 + (1 - core) * 512, 512), 512)]
            dst = r0.at[c]
            target = device(1 - core, at)
        else:
            axis = order[stage - 1]
            other = moved(at, axis, d)
            index = [at[a] if a in order[:stage - 1] else slice(None) for a in range(3)]
            index[axis] = other[axis]
            src = mine.at[(c,) + tuple(index)]
            dst = lands[stage].at[c, d - 1]
            target = device(core, other)
        return pltpu.make_async_remote_copy(
            src_ref=src, dst_ref=dst, send_sem=ss_sem.at[c, stage, d - 1],
            recv_sem=sr_sem.at[c, stage, d - 1], device_id=target, device_id_type=MESH)

    def s_each(stage):
        return (1, 3, 2) if stage else (1,)

    def s_take(c, o, stage):
        for d in s_each(stage):
            s_copy(c, o, stage, d).wait_recv()
        if stage == 0:
            total = part[pl.ds(pl.multiple_of(c * 1024 + core * 512, 512), 512), :] + r0[c]
            mine[c] = total.reshape(4, 4, 4, 8, 128)
            return
        index = (c,) + tuple(at[a] if a in ORDERS[o][:stage] else slice(None) for a in range(3))
        total = mine[index]
        for d in (1, 2, 3):
            total += lands[stage][c, d - 1]
        if stage == 3:
            final[pl.ds(pl.multiple_of(c * 8, 8), 8), :] = total
        else:
            mine[index] = total

    def s_advance(c, stage):
        for o in range(3):
            @pl.when(jnp.logical_and(jnp.logical_and(c >= 0, c < CHUNKS), c % 3 == o))
            def _():
                if stage:
                    s_take(c, o, stage - 1)
                if stage < 4:
                    for d in s_each(stage):
                        s_copy(c, o, stage, d).start()

    def fetch(b):
        return pltpu.make_async_copy(img.at[pl.ds(b * 4096, 4096)], raw.at[b % 2], img_sem.at[b % 2])

    def relayout(b):
        if b < 7:
            fetch(b + 1).start()
        fetch(b).wait()
        wide[pl.ds(0, 4096)] = raw[b % 2].astype(F32)

        @pl.loop(0, ROWS)
        def _(r):
            lanes = pl.ds(pl.multiple_of(r * 128, 128), 128)
            x[pl.ds(b * 64, 64), lanes] = wide[pl.ds(r, 64, stride=ROWS), :].astype(BF16)

    def choose():
        ids = lax.broadcasted_iota(jnp.int32, (128, 128), 0)
        pick = jnp.where(ids == tid[...], 1.0, 0.0).astype(BF16)
        shifts_t = jnp.dot(table[...].astype(F32).astype(BF16), pick, preferred_element_type=F32)
        slot = lax.broadcasted_iota(jnp.int32, (128, 128), 1)
        row, col = slot // 16, slot % 16
        inner = (col % 2) * 64 + (row % 4) * 16 + ((col // 8) * 2 + row // 4) * 4 + (col // 2) % 4
        perm = jnp.where(ids == inner, 1.0, 0.0).astype(BF16)
        shifts = lax.dot_general(perm, shifts_t.astype(BF16), (((1,), (1,)), ((), ())),
                                 preferred_element_type=F32)
        lane = lax.broadcasted_iota(jnp.int32, (128, 64), 1).astype(F32)
        odd_lane = jnp.where((lax.broadcasted_iota(jnp.int32, (128, 64), 1) // 8) % 2 == 1, 1.0, 0.0)
        for j in range(SHIFTS):
            one = jnp.where(lane == shifts[:, j:j + 1], 1.0, 0.0)
            odd = jnp.sum(one * odd_lane, axis=1, keepdims=True)
            sign[pl.ds(j * 128, 128), :] = jnp.broadcast_to(1.0 - 2.0 * odd, (128, 128))
            one = one.astype(BF16)
            onehot[pl.ds(j * 128, 128), :] = jnp.concatenate([one, one, one], axis=1)

    def widen(half):
        @pl.loop(0, 16)
        def _(i):
            for k in range(4):
                rows = pl.ds(pl.multiple_of((half * 64 + i * 4 + k) * ROWS, ROWS), ROWS)
                wide[rows] = got[half, i // 4, i % 4, k].astype(F32)

    tab_copy = pltpu.make_async_copy(tab, tabs, tab_sem)
    fetch(0).start()
    tab_copy.start()
    enter(core, at)
    got[core, at[0], at[1], at[2]] = own_t[...]
    g_stage(0)
    choose()
    norm[...] = jnp.zeros_like(norm)
    acc[...] = jnp.zeros_like(acc)
    relayout(0)
    relayout(1)
    g_stage(1)
    for b in (2, 3, 4):
        relayout(b)
    g_stage(2)
    for b in (5, 6, 7):
        relayout(b)
    g_stage(3)
    widen(core)
    tab_copy.wait()
    for k in range(4):
        lanes = slice(k * 1024, k * 1024 + 1024)
        fac[:, lanes] = jnp.dot(onehot[...], tabs[:, lanes], preferred_element_type=F32)
    g_stage(4)
    widen(1 - core)

    def factor(q, rows, tile):
        start = pl.multiple_of((q % HALF_STEPS) * STEP + tile * 256, 256)
        return fac[rows, pl.ds(start, 128)], fac[rows, pl.ds(start + 128, 128)]

    def rotate(q, rot):
        count = jnp.where(q < STEPS, 1.0, 0.0)
        for b in range(TEMPLATES // RB):
            squares = jnp.zeros((RB, 128), F32)
            for tile in range(2):
                r = b * RB * ROWS + ((q + HALF_STEPS) % STEPS) * 4 + 2 * tile
                re = wide[pl.ds(r, RB, stride=ROWS), :]
                im = wide[pl.ds(r + 1, RB, stride=ROWS), :]
                squares += re * re + im * im
                for j in range(SHIFTS):
                    rows = pl.ds(j * 128 + b * RB, RB)
                    c, s = factor(q, rows, tile)
                    rot[rows, tile * 256:tile * 256 + 128] = (re * c + im * s).astype(BF16)
                    rot[rows, tile * 256 + 128:tile * 256 + 256] = (im * c - re * s).astype(BF16)
            norm[b * RB:b * RB + RB, :] += squares * count

    def images(q):
        return x[:, pl.ds(pl.multiple_of((q % STEPS) * STEP, STEP), STEP)]

    def add_scores(q, rot):
        acc[...] += lax.dot_general(rot[...], images(q + HALF_STEPS), (((1,), (1,)), ((), ())),
                                    preferred_element_type=F32)

    def four(value):
        return jnp.concatenate([value] * 4, axis=1)

    rotate(0, rot_a)

    @pl.loop(0, 2)
    def _(half):
        @pl.loop(0, PAIRS // 32)
        def _(i):
            rows = pl.ds(pl.multiple_of(i * 32, 32), 32)
            acc[rows, :] *= four(sign[rows, :])

        @pl.loop(0, HALF_STEPS // 2)
        def _(i):
            q = half * HALF_STEPS + 2 * i
            add_scores(q, rot_a)
            rotate(q + 1, rot_b)
            add_scores(q + 1, rot_b)
            rotate(q + 2, rot_a)

    precision = prec[...]
    norm[...] = jnp.broadcast_to(0.5 * jnp.sum(norm[...], axis=1, keepdims=True), (TEMPLATES, 128))

    def score(i, top):
        rows = pl.ds(pl.multiple_of(i * 8, 8), 8)
        half = norm[pl.ds(pl.multiple_of((i % 16) * 8, 8), 8), :]
        value = precision * (acc[rows, :] - four(half))
        acc[rows, :] = value
        return jnp.maximum(top, value)

    top = lax.fori_loop(0, PAIRS // 8, score, jnp.full((8, N_IMG), -jnp.inf, F32), unroll=4)
    top = jnp.max(top, axis=0, keepdims=True)

    def exponent(i, total):
        rows = pl.ds(pl.multiple_of(i * 8, 8), 8)
        value = jnp.exp(acc[rows, :] - top)
        acc[rows, :] = value
        return total + value

    total = lax.fori_loop(0, PAIRS // 8, exponent, jnp.zeros((8, N_IMG), F32), unroll=4)
    scale = 1.0 / jnp.sum(total, axis=0, keepdims=True)

    @pl.loop(0, TEMPLATES // 16)
    def _(b):
        total = jnp.zeros((16, 128), F32)
        for j in range(SHIFTS):
            rows = pl.ds(pl.multiple_of(j * 128 + b * 16, 16), 16)
            weight = (acc[rows, :] * scale).astype(BF16)
            wts[0, rows, :] = weight
            weight = weight.astype(F32)
            wts[1, rows, :] = (weight * four(sign[rows, :])).astype(BF16)
            for lanes in range(4):
                total += weight[:, lanes * 128:lanes * 128 + 128]
        part[pl.ds(b * 128, 16, stride=8), :] = total
        for r in range(1, 8):
            part[pl.ds(b * 128 + r, 16, stride=8), :] = jnp.zeros((16, 128), F32)

    s_advance(jnp.int32(0), 0)

    def gather_images(q, buf):
        buf[...] = jnp.dot(wts[(q // HALF_STEPS) % 2], images(q), preferred_element_type=F32)

    def turn_back(q, buf, chunk, odd):
        for b in range(TEMPLATES // BB):
            for tile in range(2):
                back_re = jnp.zeros((BB, 128), F32)
                back_im = jnp.zeros((BB, 128), F32)
                for j in range(SHIFTS):
                    rows = pl.ds(j * 128 + b * BB, BB)
                    c, s = factor(q, rows, tile)
                    re = buf[rows, tile * 256:tile * 256 + 128]
                    im = buf[rows, tile * 256 + 128:tile * 256 + 256]
                    back_re += re * c - im * s
                    back_im += im * c + re * s
                r = chunk * 1024 + b * BB * 8 + odd * 4 + 2 * tile
                part[pl.ds(r, BB, stride=8), :] = back_re
                part[pl.ds(r + 1, BB, stride=8), :] = back_im

    gather_images(jnp.int32(0), buf_a)

    @pl.loop(0, STEPS // 2)
    def _(i):
        gather_images(2 * i + 1, buf_b)
        turn_back(2 * i, buf_a, i + 1, 0)
        gather_images(2 * i + 2, buf_a)
        turn_back(2 * i + 1, buf_b, i + 1, 1)
        for stage in range(5):
            s_advance(i + 1 - stage, stage)

    @pl.loop(CHUNKS, CHUNKS + 4)
    def _(i):
        for stage in range(1, 5):
            s_advance(i - stage, stage)

    @pl.loop(0, CHUNKS // 3)
    def _(i):
        for o in range(3):
            for stage in range(4):
                for d in s_each(stage):
                    s_copy(i * 3 + o, o, stage, d).wait_send()
    for stage in range(4):
        for g in range(4):
            for d in g_each(stage):
                g_copy(g, stage, d).wait_send()

    total = jnp.sum(final[0:8, :], keepdims=True) + PRIOR_WEIGHT
    out_ref[...] = (final[8:72, :] + PRIOR_WEIGHT * own_t[...].astype(F32)) / total


def body(images, precision, templates, template_id, shift_table):
    vmem = pl.BlockSpec(memory_space=pltpu.VMEM)
    anywhere = pl.BlockSpec(memory_space=pl.ANY)
    dma = pltpu.SemaphoreType.DMA
    img = images.reshape(N_IMG, 2, 32, 128).transpose(0, 2, 1, 3).reshape(N_IMG * ROWS, 128)
    own = templates.reshape(2, 32, 128).transpose(1, 0, 2).reshape(ROWS, 128)
    tab = jnp.asarray(phase_constant())
    out = pl.pallas_call(
        em_kernel,
        out_shape=jax.ShapeDtypeStruct((ROWS, 128), F32),
        in_specs=[anywhere, anywhere, vmem, vmem, vmem, vmem], out_specs=vmem,
        scratch_shapes=[
            pltpu.VMEM((N_IMG, 2 * COEFFS), BF16),
            pltpu.VMEM((2, 4096, 128), BF16),
            pltpu.VMEM((TEMPLATES * ROWS, 128), F32),
            pltpu.VMEM((PAIRS, COEFFS), F32),
            pltpu.VMEM((PAIRS, N_IMG), F32),
            pltpu.VMEM((PAIRS, STEP), BF16),
            pltpu.VMEM((PAIRS, STEP), BF16),
            pltpu.VMEM((PAIRS, STEP), F32),
            pltpu.VMEM((PAIRS, STEP), F32),
            pltpu.VMEM((2, PAIRS, N_IMG), BF16),
            pltpu.VMEM((PAIRS, 192), BF16),
            pltpu.VMEM((PAIRS, 128), F32),
            pltpu.VMEM((TEMPLATES, 128), F32),
            pltpu.VMEM((192, COEFFS), BF16),
            pltpu.VMEM((2, 4, 4, 4, ROWS, 128), BF16),
            pltpu.VMEM((CHUNKS * 1024, 128), F32),
            pltpu.VMEM((CHUNKS, 512, 128), F32),
            pltpu.VMEM((CHUNKS, 4, 4, 4, 8, 128), F32),
            pltpu.VMEM((CHUNKS, 3, 4, 4, 8, 128), F32),
            pltpu.VMEM((CHUNKS, 3, 4, 8, 128), F32),
            pltpu.VMEM((CHUNKS, 3, 8, 128), F32),
            pltpu.VMEM((72, 128), F32),
            dma((2,)), dma, dma((4, 4, 3)), dma((4, 4, 3)),
            dma((CHUNKS, 4, 3)), dma((CHUNKS, 4, 3)),
        ],
        compiler_params=pltpu.CompilerParams(collective_id=0, has_side_effects=True,
                                             vmem_limit_bytes=60 * MIB),
        name="em_step",
    )(img, tab, own, precision.reshape(1, N_IMG), template_id.reshape(1, TEMPLATES), shift_table.T)
    return out.reshape(32, 2, 128).transpose(1, 0, 2).reshape(1, 2, COEFFS)


def solution(mesh):
    return jax.shard_map(
        body,
        mesh=mesh,
        in_specs=(
            P(("row", "col"), None, None),
            P(("row", "col")),
            P(("row", "col"), None, None),
            P(),
            P(),
        ),
        out_specs=P(("row", "col"), None, None),
        check_vma=False,
    )
```

```python
import functools

import jax
import jax.numpy as jnp
import ml_dtypes
import numpy as np
from jax import lax
from jax.experimental import pallas as pl
from jax.experimental.pallas import tpu as pltpu
from jax.sharding import PartitionSpec as P

MESH = pl.DeviceIdType.MESH
F32 = jnp.float32
BF16 = jnp.bfloat16

GRID = 64
COEFFS = 4096
TEMPLATES = 128
SHIFTS = 8
PAIRS = TEMPLATES * SHIFTS
N_IMG = 512
ROWS = 64
STEP = 512
STEPS = 2 * COEFFS // STEP
HALF_STEPS = STEPS // 2
PITCH = 65
LAG = (0, 2, 6, 9, 11)
CHUNKS = 9
PRIOR_WEIGHT = 4.0
RB, BB = 32, 16
MIB = 1 << 20

ORDERS = ((2, 1, 0), (1, 0, 2), (0, 2, 1))


def phase_constant():
    c = np.arange(COEFFS)
    fx = c // GRID - GRID // 2
    fy = c % GRID - GRID // 2
    s = np.arange(64)
    k = ((s // 8 - 4)[:, None] * fx[None] + (s % 8 - 4)[:, None] * fy[None]) % GRID
    angle = k * (2.0 * np.pi / GRID)
    both = np.stack([np.cos(angle), np.sin(angle)], 1).reshape(64, 2, 32, 128)
    both = both.transpose(0, 2, 1, 3).reshape(64, 2 * COEFFS)[:, :COEFFS].astype(np.float32)
    high = both.astype(ml_dtypes.bfloat16)
    rest = both - high.astype(np.float32)
    mid = rest.astype(ml_dtypes.bfloat16)
    low = (rest - mid.astype(np.float32)).astype(ml_dtypes.bfloat16)
    return np.concatenate([high, mid, low], 0)


def place():
    row, col = lax.axis_index("row"), lax.axis_index("col")
    z, y_lo = row % 4, row // 4
    core, x, y_hi = col % 2, (col // 2) % 4, col // 8
    return core, (z, y_hi * 2 + y_lo, x)


def device(core, at):
    z, y, x = at
    return ((y % 2) * 4 + z, ((y // 2) * 4 + x) * 2 + core)


def moved(at, axis, by):
    return tuple((v + by) % 4 if i == axis else v for i, v in enumerate(at))


def enter(core, at):
    barrier = pltpu.get_barrier_semaphore()
    others = [device(1 - core, at)]
    others += [device(core, moved(at, a, d)) for a in range(3) for d in (1, 2, 3)]
    for other in others:
        pl.semaphore_signal(barrier, inc=1, device_id=other, device_id_type=MESH)
    pl.semaphore_wait(barrier, len(others))


def em_kernel(img, tab, own_t, prec, tid, table, out_ref,
              x, raw, wide, fac, acc, rot_a, rot_b, buf_a, buf_b, wts, onehot, sign, norm, tabs,
              got, part, r0, mine, r1, r2, r3, final,
              img_sem, tab_sem, gs_sem, gr_sem, ss_sem, sr_sem):
    core, at = place()

    groups = [(pl.ds(16 * g, 16), (ORDERS + ORDERS)[g]) for g in range(4)]

    def view(rows, order, stage, where):
        done = order[:stage]
        index = tuple(slice(None) if a in done else where[a] for a in range(3))
        return got.at[(core,) + index + (rows,)]

    def g_copy(g, stage, d, arrived=False):
        rows, order = groups[g]
        if stage == 3:
            ref = got.at[1 - core if arrived else core, :, :, :, rows]
            target = device(1 - core, at)
        else:
            axis = order[stage]
            ref = view(rows, order, stage, moved(at, axis, 4 - d) if arrived else at)
            target = device(core, moved(at, axis, d))
        return pltpu.make_async_remote_copy(
            src_ref=ref, dst_ref=ref, send_sem=gs_sem.at[g, stage, d - 1],
            recv_sem=gr_sem.at[g, stage, d - 1], device_id=target, device_id_type=MESH)

    def g_each(stage):
        return (1, 3, 2) if stage < 3 else (1,)

    def g_stage(stage):
        for g in range(4):
            if stage:
                for d in g_each(stage - 1):
                    g_copy(g, stage - 1, d, True).wait_recv()
            if stage < 4:
                for d in g_each(stage):
                    g_copy(g, stage, d).start()

    lands = (r0, r1, r2, r3)

    def s_copy(c, o, stage, d):
        order = ORDERS[o]
        if stage == 0:
            src = part.at[pl.ds(pl.multiple_of(c * 1024 + (1 - core) * 512, 512), 512)]
            dst = r0.at[c]
            target = device(1 - core, at)
        else:
            axis = order[stage - 1]
            other = moved(at, axis, d)
            index = [at[a] if a in order[:stage - 1] else slice(None) for a in range(3)]
            index[axis] = other[axis]
            src = mine.at[(c,) + tuple(index)]
            dst = lands[stage].at[c, d - 1]
            target = device(core, other)
        return pltpu.make_async_remote_copy(
            src_ref=src, dst_ref=dst, send_sem=ss_sem.at[c, stage, d - 1],
            recv_sem=sr_sem.at[c, stage, d - 1], device_id=target, device_id_type=MESH)

    def s_each(stage):
        return (1, 3, 2) if stage else (1,)

    def s_take(c, o, stage):
        for d in s_each(stage):
            s_copy(c, o, stage, d).wait_recv()
        if stage == 0:
            total = part[pl.ds(pl.multiple_of(c * 1024 + core * 512, 512), 512), :] + r0[c]
            mine[c] = total.reshape(4, 4, 4, 8, 128)
            return
        index = (c,) + tuple(at[a] if a in ORDERS[o][:stage] else slice(None) for a in range(3))
        total = mine[index]
        for d in (1, 2, 3):
            total += lands[stage][c, d - 1]
        if stage == 3:
            final[pl.ds(pl.multiple_of(c * 8, 8), 8), :] = total
        else:
            mine[index] = total

    def s_advance(c, stage):
        for o in range(3):
            @pl.when(jnp.logical_and(jnp.logical_and(c >= 0, c < CHUNKS), c % 3 == o))
            def _():
                if stage:
                    s_take(c, o, stage - 1)
                if stage < 4:
                    for d in s_each(stage):
                        s_copy(c, o, stage, d).start()

    def fetch(b):
        return pltpu.make_async_copy(img.at[pl.ds(b * 4096, 4096)], raw.at[b % 2], img_sem.at[b % 2])

    def relayout(b):
        if b < 7:
            fetch(b + 1).start()
        fetch(b).wait()

        @pl.loop(0, 8)
        def _(i):
            for k in range(8):
                n = i * 8 + k
                rows = pl.ds(pl.multiple_of(n * ROWS, ROWS), ROWS)
                wide[pl.ds(n * PITCH, ROWS)] = raw[b % 2, rows].astype(F32)

        @pl.loop(0, ROWS // 8)
        def _(i):
            for k in range(8):
                r = i * 8 + k
                lanes = pl.ds(pl.multiple_of(r * 128, 128), 128)
                x[pl.ds(b * 64, 64), lanes] = wide[pl.ds(r, 64, stride=PITCH), :].astype(BF16)

    def choose():
        ids = lax.broadcasted_iota(jnp.int32, (128, 128), 0)
        pick = jnp.where(ids == tid[...], 1.0, 0.0).astype(BF16)
        shifts_t = jnp.dot(table[...].astype(F32).astype(BF16), pick, preferred_element_type=F32)
        slot = lax.broadcasted_iota(jnp.int32, (128, 128), 1)
        row, col = slot // 16, slot % 16
        inner = (col % 2) * 64 + (row % 4) * 16 + ((col // 8) * 2 + row // 4) * 4 + (col // 2) % 4
        perm = jnp.where(ids == inner, 1.0, 0.0).astype(BF16)
        shifts = lax.dot_general(perm, shifts_t.astype(BF16), (((1,), (1,)), ((), ())),
                                 preferred_element_type=F32)
        lane = lax.broadcasted_iota(jnp.int32, (128, 64), 1).astype(F32)
        odd_lane = jnp.where((lax.broadcasted_iota(jnp.int32, (128, 64), 1) // 8) % 2 == 1, 1.0, 0.0)
        for j in range(SHIFTS):
            one = jnp.where(lane == shifts[:, j:j + 1], 1.0, 0.0)
            odd = jnp.sum(one * odd_lane, axis=1, keepdims=True)
            sign[pl.ds(j * 128, 128), :] = jnp.broadcast_to(1.0 - 2.0 * odd, (128, 128))
            one = one.astype(BF16)
            onehot[pl.ds(j * 128, 128), :] = jnp.concatenate([one, one, one], axis=1)

    def widen(half):
        @pl.loop(0, 16)
        def _(i):
            for k in range(4):
                rows = pl.ds((half * 64 + i * 4 + k) * PITCH, ROWS)
                wide[rows] = got[half, i // 4, i % 4, k].astype(F32)

    tab_copy = pltpu.make_async_copy(tab, tabs, tab_sem)
    fetch(0).start()
    tab_copy.start()
    enter(core, at)
    got[core, at[0], at[1], at[2]] = own_t[...]
    g_stage(0)
    choose()
    norm[...] = jnp.zeros_like(norm)
    acc[...] = jnp.zeros_like(acc)
    relayout(0)
    relayout(1)
    g_stage(1)
    for b in (2, 3, 4):
        relayout(b)
    g_stage(2)
    for b in (5, 6, 7):
        relayout(b)
    g_stage(3)
    widen(core)
    tab_copy.wait()
    for k in range(4):
        lanes = slice(k * 1024, k * 1024 + 1024)
        fac[:, lanes] = jnp.dot(onehot[...], tabs[:, lanes], preferred_element_type=F32)
    g_stage(4)
    widen(1 - core)

    def factor(q, rows, tile):
        start = pl.multiple_of((q % HALF_STEPS) * STEP + tile * 256, 256)
        return fac[rows, pl.ds(start, 128)], fac[rows, pl.ds(start + 128, 128)]

    def rotate(q, rot):
        count = jnp.where(q < STEPS, 1.0, 0.0)
        for b in range(TEMPLATES // RB):
            squares = jnp.zeros((RB, 128), F32)
            for tile in range(2):
                r = b * RB * PITCH + ((q + HALF_STEPS) % STEPS) * 4 + 2 * tile
                re = wide[pl.ds(r, RB, stride=PITCH), :]
                im = wide[pl.ds(r + 1, RB, stride=PITCH), :]
                squares += re * re + im * im
                for j in range(SHIFTS):
                    rows = pl.ds(j * 128 + b * RB, RB)
                    c, s = factor(q, rows, tile)
                    rot[rows, tile * 256:tile * 256 + 128] = (re * c + im * s).astype(BF16)
                    rot[rows, tile * 256 + 128:tile * 256 + 256] = (im * c - re * s).astype(BF16)
            norm[b * RB:b * RB + RB, :] += squares * count

    def images(q):
        return x[:, pl.ds(pl.multiple_of((q % STEPS) * STEP, STEP), STEP)]

    def add_scores(q, rot):
        acc[...] += lax.dot_general(rot[...], images(q + HALF_STEPS), (((1,), (1,)), ((), ())),
                                    preferred_element_type=F32)

    def four(value):
        return jnp.concatenate([value] * 4, axis=1)

    rotate(0, rot_a)

    @pl.loop(0, 2)
    def _(half):
        @pl.loop(0, PAIRS // 32)
        def _(i):
            rows = pl.ds(pl.multiple_of(i * 32, 32), 32)
            acc[rows, :] *= four(sign[rows, :])

        @pl.loop(0, HALF_STEPS // 2)
        def _(i):
            q = half * HALF_STEPS + 2 * i
            add_scores(q, rot_a)
            rotate(q + 1, rot_b)
            add_scores(q + 1, rot_b)
            rotate(q + 2, rot_a)

    precision = prec[...]
    norm[...] = jnp.broadcast_to(0.5 * jnp.sum(norm[...], axis=1, keepdims=True), (TEMPLATES, 128))

    def score(i, top):
        rows = pl.ds(pl.multiple_of(i * 8, 8), 8)
        half = norm[pl.ds(pl.multiple_of((i % 16) * 8, 8), 8), :]
        value = precision * (acc[rows, :] - four(half))
        acc[rows, :] = value
        return jnp.maximum(top, value)

    top = lax.fori_loop(0, PAIRS // 8, score, jnp.full((8, N_IMG), -jnp.inf, F32), unroll=4)
    top = jnp.max(top, axis=0, keepdims=True)

    def exponent(i, total):
        rows = pl.ds(pl.multiple_of(i * 8, 8), 8)
        value = jnp.exp(acc[rows, :] - top)
        acc[rows, :] = value
        return total + value

    total = lax.fori_loop(0, PAIRS // 8, exponent, jnp.zeros((8, N_IMG), F32), unroll=4)
    scale = 1.0 / jnp.sum(total, axis=0, keepdims=True)

    @pl.loop(0, TEMPLATES // 16)
    def _(b):
        total = jnp.zeros((16, 128), F32)
        for j in range(SHIFTS):
            rows = pl.ds(pl.multiple_of(j * 128 + b * 16, 16), 16)
            weight = (acc[rows, :] * scale).astype(BF16)
            wts[0, rows, :] = weight
            weight = weight.astype(F32)
            wts[1, rows, :] = (weight * four(sign[rows, :])).astype(BF16)
            for lanes in range(4):
                total += weight[:, lanes * 128:lanes * 128 + 128]
        part[pl.ds(b * 128, 16, stride=8), :] = total
        for r in range(1, 8):
            part[pl.ds(b * 128 + r, 16, stride=8), :] = jnp.zeros((16, 128), F32)

    s_advance(jnp.int32(0), 0)

    def gather_images(q, buf):
        buf[...] = jnp.dot(wts[(q // HALF_STEPS) % 2], images(q), preferred_element_type=F32)

    def turn_back(q, buf, chunk, odd):
        for b in range(TEMPLATES // BB):
            for tile in range(2):
                back_re = jnp.zeros((BB, 128), F32)
                back_im = jnp.zeros((BB, 128), F32)
                for j in range(SHIFTS):
                    rows = pl.ds(j * 128 + b * BB, BB)
                    c, s = factor(q, rows, tile)
                    re = buf[rows, tile * 256:tile * 256 + 128]
                    im = buf[rows, tile * 256 + 128:tile * 256 + 256]
                    back_re += re * c - im * s
                    back_im += im * c + re * s
                r = chunk * 1024 + b * BB * 8 + odd * 4 + 2 * tile
                part[pl.ds(r, BB, stride=8), :] = back_re
                part[pl.ds(r + 1, BB, stride=8), :] = back_im

    gather_images(jnp.int32(0), buf_a)

    @pl.loop(0, STEPS // 2)
    def _(i):
        gather_images(2 * i + 1, buf_b)
        turn_back(2 * i, buf_a, i + 1, 0)
        gather_images(2 * i + 2, buf_a)
        turn_back(2 * i + 1, buf_b, i + 1, 1)
        for stage in range(5):
            s_advance(i + 1 - LAG[stage], stage)

    @pl.loop(CHUNKS, CHUNKS + LAG[4])
    def _(i):
        for stage in range(1, 5):
            s_advance(i - LAG[stage], stage)

    @pl.loop(0, CHUNKS // 3)
    def _(i):
        for o in range(3):
            for stage in range(4):
                for d in s_each(stage):
                    s_copy(i * 3 + o, o, stage, d).wait_send()
    for stage in range(4):
        for g in range(4):
            for d in g_each(stage):
                g_copy(g, stage, d).wait_send()

    total = jnp.sum(final[0:8, :], keepdims=True) + PRIOR_WEIGHT
    out_ref[...] = (final[8:72, :] + PRIOR_WEIGHT * own_t[...].astype(F32)) / total


def body(images, precision, templates, template_id, shift_table):
    vmem = pl.BlockSpec(memory_space=pltpu.VMEM)
    anywhere = pl.BlockSpec(memory_space=pl.ANY)
    dma = pltpu.SemaphoreType.DMA
    img = images.reshape(N_IMG, 2, 32, 128).transpose(0, 2, 1, 3).reshape(N_IMG * ROWS, 128)
    own = templates.reshape(2, 32, 128).transpose(1, 0, 2).reshape(ROWS, 128)
    tab = jnp.asarray(phase_constant())
    out = pl.pallas_call(
        em_kernel,
        out_shape=jax.ShapeDtypeStruct((ROWS, 128), F32),
        in_specs=[anywhere, anywhere, vmem, vmem, vmem, vmem], out_specs=vmem,
        scratch_shapes=[
            pltpu.VMEM((N_IMG, 2 * COEFFS), BF16),
            pltpu.VMEM((2, 4096, 128), BF16),
            pltpu.VMEM((TEMPLATES * PITCH, 128), F32),
            pltpu.VMEM((PAIRS, COEFFS), F32),
            pltpu.VMEM((PAIRS, N_IMG), F32),
            pltpu.VMEM((PAIRS, STEP), BF16),
            pltpu.VMEM((PAIRS, STEP), BF16),
            pltpu.VMEM((PAIRS, STEP), F32),
            pltpu.VMEM((PAIRS, STEP), F32),
            pltpu.VMEM((2, PAIRS, N_IMG), BF16),
            pltpu.VMEM((PAIRS, 192), BF16),
            pltpu.VMEM((PAIRS, 128), F32),
            pltpu.VMEM((TEMPLATES, 128), F32),
            pltpu.VMEM((192, COEFFS), BF16),
            pltpu.VMEM((2, 4, 4, 4, ROWS, 128), BF16),
            pltpu.VMEM((CHUNKS * 1024, 128), F32),
            pltpu.VMEM((CHUNKS, 512, 128), F32),
            pltpu.VMEM((CHUNKS, 4, 4, 4, 8, 128), F32),
            pltpu.VMEM((CHUNKS, 3, 4, 4, 8, 128), F32),
            pltpu.VMEM((CHUNKS, 3, 4, 8, 128), F32),
            pltpu.VMEM((CHUNKS, 3, 8, 128), F32),
            pltpu.VMEM((72, 128), F32),
            dma((2,)), dma, dma((4, 4, 3)), dma((4, 4, 3)),
            dma((CHUNKS, 4, 3)), dma((CHUNKS, 4, 3)),
        ],
        compiler_params=pltpu.CompilerParams(collective_id=0, has_side_effects=True,
                                             vmem_limit_bytes=60 * MIB),
        name="em_step",
    )(img, tab, own, precision.reshape(1, N_IMG), template_id.reshape(1, TEMPLATES), shift_table.T)
    return out.reshape(32, 2, 128).transpose(1, 0, 2).reshape(1, 2, COEFFS)


def solution(mesh):
    return jax.shard_map(
        body,
        mesh=mesh,
        in_specs=(
            P(("row", "col"), None, None),
            P(("row", "col")),
            P(("row", "col"), None, None),
            P(),
            P(),
        ),
        out_specs=P(("row", "col"), None, None),
        check_vma=False,
    )
```

```python
import functools

import jax
import jax.numpy as jnp
import ml_dtypes
import numpy as np
from jax import lax
from jax.experimental import pallas as pl
from jax.experimental.pallas import tpu as pltpu
from jax.sharding import PartitionSpec as P

MESH = pl.DeviceIdType.MESH
F32 = jnp.float32
BF16 = jnp.bfloat16

GRID = 64
COEFFS = 4096
TEMPLATES = 128
SHIFTS = 8
PAIRS = TEMPLATES * SHIFTS
N_IMG = 512
ROWS = 64
STEP = 512
STEPS = 2 * COEFFS // STEP
HALF_STEPS = STEPS // 2
PITCH = 65
LAG = (0, 2, 7, 11, 13)
CHUNKS = 9
PRIOR_WEIGHT = 4.0
RB, BB = 32, 16
MIB = 1 << 20

ORDERS = ((2, 1, 0), (1, 0, 2), (0, 2, 1))


def phase_constant():
    c = np.arange(COEFFS)
    fx = c // GRID - GRID // 2
    fy = c % GRID - GRID // 2
    s = np.arange(64)
    k = ((s // 8 - 4)[:, None] * fx[None] + (s % 8 - 4)[:, None] * fy[None]) % GRID
    angle = k * (2.0 * np.pi / GRID)
    both = np.stack([np.cos(angle), np.sin(angle)], 1).reshape(64, 2, 32, 128)
    both = both.transpose(0, 2, 1, 3).reshape(64, 2 * COEFFS)[:, :COEFFS].astype(np.float32)
    high = both.astype(ml_dtypes.bfloat16)
    rest = both - high.astype(np.float32)
    mid = rest.astype(ml_dtypes.bfloat16)
    low = (rest - mid.astype(np.float32)).astype(ml_dtypes.bfloat16)
    return np.concatenate([high, mid, low], 0)


def place():
    row, col = lax.axis_index("row"), lax.axis_index("col")
    z, y_lo = row % 4, row // 4
    core, x, y_hi = col % 2, (col // 2) % 4, col // 8
    return core, (z, y_hi * 2 + y_lo, x)


def device(core, at):
    z, y, x = at
    return ((y % 2) * 4 + z, ((y // 2) * 4 + x) * 2 + core)


def moved(at, axis, by):
    return tuple((v + by) % 4 if i == axis else v for i, v in enumerate(at))


def enter(core, at):
    barrier = pltpu.get_barrier_semaphore()
    others = [device(1 - core, at)]
    others += [device(core, moved(at, a, d)) for a in range(3) for d in (1, 2, 3)]
    for other in others:
        pl.semaphore_signal(barrier, inc=1, device_id=other, device_id_type=MESH)
    pl.semaphore_wait(barrier, len(others))


def em_kernel(img, tab, own_t, prec, tid, table, out_ref,
              x, raw, wide, fac, acc, rot_a, rot_b, buf_a, buf_b, wts, onehot, sign, norm, tabs,
              got, part, r0, mine, r1, r2, r3, final,
              img_sem, tab_sem, gs_sem, gr_sem, ss_sem, sr_sem):
    core, at = place()

    groups = [(pl.ds(16 * g, 16), (ORDERS + ORDERS)[g]) for g in range(4)]

    def view(rows, order, stage, where):
        done = order[:stage]
        index = tuple(slice(None) if a in done else where[a] for a in range(3))
        return got.at[(core,) + index + (rows,)]

    def g_copy(g, stage, d):
        rows, order = groups[g]
        if stage == 3:
            ref = got.at[core, :, :, :, rows]
            target = device(1 - core, at)
        else:
            ref = view(rows, order, stage, at)
            target = device(core, moved(at, order[stage], d))
        return pltpu.make_async_remote_copy(
            src_ref=ref, dst_ref=ref, send_sem=gs_sem, recv_sem=gr_sem.at[g, stage],
            device_id=target, device_id_type=MESH)

    def await_bytes(ref, sem):
        pltpu.make_async_copy(ref, ref, sem).wait()

    def g_each(stage):
        return (1, 3, 2) if stage < 3 else (1,)

    def g_stage(stage):
        for g in range(4):
            if stage:
                await_bytes(raw.at[0, pl.ds(0, 16 * (3, 12, 48, 64)[stage - 1])], gr_sem.at[g, stage - 1])
            if stage < 4:
                for d in g_each(stage):
                    g_copy(g, stage, d).start()

    lands = (r0, r1, r2, r3)

    def s_copy(c, o, stage, d):
        order = ORDERS[o]
        if stage == 0:
            src = part.at[pl.ds(pl.multiple_of(c * 1024 + (1 - core) * 512, 512), 512)]
            dst = r0.at[c]
            target = device(1 - core, at)
        else:
            axis = order[stage - 1]
            other = moved(at, axis, d)
            index = [at[a] if a in order[:stage - 1] else slice(None) for a in range(3)]
            index[axis] = other[axis]
            src = mine.at[(c,) + tuple(index)]
            dst = lands[stage].at[c, d - 1]
            target = device(core, other)
        return pltpu.make_async_remote_copy(
            src_ref=src, dst_ref=dst, send_sem=ss_sem,
            recv_sem=sr_sem.at[c, stage], device_id=target, device_id_type=MESH)

    def s_each(stage):
        return (1, 3, 2) if stage else (1,)

    def s_take(c, o, stage):
        await_bytes(lands[stage].at[c], sr_sem.at[c, stage])
        if stage == 0:
            total = part[pl.ds(pl.multiple_of(c * 1024 + core * 512, 512), 512), :] + r0[c]
            mine[c] = total.reshape(4, 4, 4, 8, 128)
            return
        index = (c,) + tuple(at[a] if a in ORDERS[o][:stage] else slice(None) for a in range(3))
        total = mine[index]
        for d in (1, 2, 3):
            total += lands[stage][c, d - 1]
        if stage == 3:
            final[pl.ds(pl.multiple_of(c * 8, 8), 8), :] = total
        else:
            mine[index] = total

    def s_advance(c, stage):
        @pl.when(jnp.logical_and(c >= 0, c < CHUNKS))
        def _():
            for o in range(3):
                @pl.when(c % 3 == o)
                def _():
                    if stage:
                        s_take(c, o, stage - 1)
                    if stage < 4:
                        for d in s_each(stage):
                            s_copy(c, o, stage, d).start()

    def fetch(b):
        return pltpu.make_async_copy(img.at[pl.ds(b * 4096, 4096)], raw.at[b % 2], img_sem.at[b % 2])

    def relayout(b):
        if b < 7:
            fetch(b + 1).start()
        fetch(b).wait()

        @pl.loop(0, 8)
        def _(i):
            for k in range(8):
                n = i * 8 + k
                rows = pl.ds(pl.multiple_of(n * ROWS, ROWS), ROWS)
                wide[pl.ds(n * PITCH, ROWS)] = raw[b % 2, rows].astype(F32)

        @pl.loop(0, ROWS // 8)
        def _(i):
            for k in range(8):
                r = i * 8 + k
                lanes = pl.ds(pl.multiple_of(r * 128, 128), 128)
                x[pl.ds(b * 64, 64), lanes] = wide[pl.ds(r, 64, stride=PITCH), :].astype(BF16)

    def choose():
        ids = lax.broadcasted_iota(jnp.int32, (128, 128), 0)
        pick = jnp.where(ids == tid[...], 1.0, 0.0).astype(BF16)
        shifts_t = jnp.dot(table[...].astype(F32).astype(BF16), pick, preferred_element_type=F32)
        slot = lax.broadcasted_iota(jnp.int32, (128, 128), 1)
        row, col = slot // 16, slot % 16
        inner = (col % 2) * 64 + (row % 4) * 16 + ((col // 8) * 2 + row // 4) * 4 + (col // 2) % 4
        perm = jnp.where(ids == inner, 1.0, 0.0).astype(BF16)
        shifts = lax.dot_general(perm, shifts_t.astype(BF16), (((1,), (1,)), ((), ())),
                                 preferred_element_type=F32)
        lane = lax.broadcasted_iota(jnp.int32, (128, 64), 1).astype(F32)
        odd_lane = jnp.where((lax.broadcasted_iota(jnp.int32, (128, 64), 1) // 8) % 2 == 1, 1.0, 0.0)
        for j in range(SHIFTS):
            one = jnp.where(lane == shifts[:, j:j + 1], 1.0, 0.0)
            odd = jnp.sum(one * odd_lane, axis=1, keepdims=True)
            sign[pl.ds(j * 128, 128), :] = jnp.broadcast_to(1.0 - 2.0 * odd, (128, 128))
            one = one.astype(BF16)
            onehot[pl.ds(j * 128, 128), :] = jnp.concatenate([one, one, one], axis=1)

    def widen(half):
        @pl.loop(0, 16)
        def _(i):
            for k in range(4):
                rows = pl.ds((half * 64 + i * 4 + k) * PITCH, ROWS)
                wide[rows] = got[half, i // 4, i % 4, k].astype(F32)

    tab_copy = pltpu.make_async_copy(tab, tabs, tab_sem)
    fetch(0).start()
    tab_copy.start()
    enter(core, at)
    got[core, at[0], at[1], at[2]] = own_t[...]
    g_stage(0)
    choose()
    norm[...] = jnp.zeros_like(norm)
    acc[...] = jnp.zeros_like(acc)
    relayout(0)
    relayout(1)
    g_stage(1)
    for b in (2, 3, 4):
        relayout(b)
    g_stage(2)
    for b in (5, 6, 7):
        relayout(b)
    g_stage(3)
    widen(core)
    tab_copy.wait()
    for k in range(4):
        lanes = slice(k * 1024, k * 1024 + 1024)
        fac[:, lanes] = jnp.dot(onehot[...], tabs[:, lanes], preferred_element_type=F32)
    g_stage(4)
    widen(1 - core)

    def factor(q, rows, tile):
        start = pl.multiple_of((q % HALF_STEPS) * STEP + tile * 256, 256)
        return fac[rows, pl.ds(start, 128)], fac[rows, pl.ds(start + 128, 128)]

    def rotate(q, rot):
        count = jnp.where(q < STEPS, 1.0, 0.0)
        for b in range(TEMPLATES // RB):
            squares = jnp.zeros((RB, 128), F32)
            for tile in range(2):
                r = b * RB * PITCH + ((q + HALF_STEPS) % STEPS) * 4 + 2 * tile
                re = wide[pl.ds(r, RB, stride=PITCH), :]
                im = wide[pl.ds(r + 1, RB, stride=PITCH), :]
                squares += re * re + im * im
                for j in range(SHIFTS):
                    rows = pl.ds(j * 128 + b * RB, RB)
                    c, s = factor(q, rows, tile)
                    rot[rows, tile * 256:tile * 256 + 128] = (re * c + im * s).astype(BF16)
                    rot[rows, tile * 256 + 128:tile * 256 + 256] = (im * c - re * s).astype(BF16)
            norm[b * RB:b * RB + RB, :] += squares * count

    def images(q):
        return x[:, pl.ds(pl.multiple_of((q % STEPS) * STEP, STEP), STEP)]

    def add_scores(q, rot):
        acc[...] += lax.dot_general(rot[...], images(q + HALF_STEPS), (((1,), (1,)), ((), ())),
                                    preferred_element_type=F32)

    def four(value):
        return jnp.concatenate([value] * 4, axis=1)

    rotate(0, rot_a)

    @pl.loop(0, 2)
    def _(half):
        @pl.loop(0, PAIRS // 32)
        def _(i):
            rows = pl.ds(pl.multiple_of(i * 32, 32), 32)
            acc[rows, :] *= four(sign[rows, :])

        @pl.loop(0, HALF_STEPS // 2)
        def _(i):
            q = half * HALF_STEPS + 2 * i
            add_scores(q, rot_a)
            rotate(q + 1, rot_b)
            add_scores(q + 1, rot_b)
            rotate(q + 2, rot_a)

    precision = prec[...]
    norm[...] = jnp.broadcast_to(0.5 * jnp.sum(norm[...], axis=1, keepdims=True), (TEMPLATES, 128))

    def score(i, top):
        rows = pl.ds(pl.multiple_of(i * 8, 8), 8)
        half = norm[pl.ds(pl.multiple_of((i % 16) * 8, 8), 8), :]
        value = precision * (acc[rows, :] - four(half))
        acc[rows, :] = value
        return jnp.maximum(top, value)

    top = lax.fori_loop(0, PAIRS // 8, score, jnp.full((8, N_IMG), -jnp.inf, F32), unroll=4)
    top = jnp.max(top, axis=0, keepdims=True)

    def exponent(i, total):
        rows = pl.ds(pl.multiple_of(i * 8, 8), 8)
        value = jnp.exp(acc[rows, :] - top)
        acc[rows, :] = value
        return total + value

    total = lax.fori_loop(0, PAIRS // 8, exponent, jnp.zeros((8, N_IMG), F32), unroll=4)
    scale = 1.0 / jnp.sum(total, axis=0, keepdims=True)

    @pl.loop(0, TEMPLATES // 16)
    def _(b):
        total = jnp.zeros((16, 128), F32)
        for j in range(SHIFTS):
            rows = pl.ds(pl.multiple_of(j * 128 + b * 16, 16), 16)
            weight = (acc[rows, :] * scale).astype(BF16)
            wts[0, rows, :] = weight
            weight = weight.astype(F32)
            wts[1, rows, :] = (weight * four(sign[rows, :])).astype(BF16)
            for lanes in range(4):
                total += weight[:, lanes * 128:lanes * 128 + 128]
        part[pl.ds(b * 128, 16, stride=8), :] = total
        for r in range(1, 8):
            part[pl.ds(b * 128 + r, 16, stride=8), :] = jnp.zeros((16, 128), F32)

    s_advance(jnp.int32(0), 0)

    def gather_images(q, buf):
        buf[...] = jnp.dot(wts[(q // HALF_STEPS) % 2], images(q), preferred_element_type=F32)

    def turn_back(q, buf, chunk, odd):
        for b in range(TEMPLATES // BB):
            for tile in range(2):
                back_re = jnp.zeros((BB, 128), F32)
                back_im = jnp.zeros((BB, 128), F32)
                for j in range(SHIFTS):
                    rows = pl.ds(j * 128 + b * BB, BB)
                    c, s = factor(q, rows, tile)
                    re = buf[rows, tile * 256:tile * 256 + 128]
                    im = buf[rows, tile * 256 + 128:tile * 256 + 256]
                    back_re += re * c - im * s
                    back_im += im * c + re * s
                r = chunk * 1024 + b * BB * 8 + odd * 4 + 2 * tile
                part[pl.ds(r, BB, stride=8), :] = back_re
                part[pl.ds(r + 1, BB, stride=8), :] = back_im

    gather_images(jnp.int32(0), buf_a)

    @pl.loop(0, STEPS // 2)
    def _(i):
        gather_images(2 * i + 1, buf_b)
        turn_back(2 * i, buf_a, i + 1, 0)
        gather_images(2 * i + 2, buf_a)
        turn_back(2 * i + 1, buf_b, i + 1, 1)
        for stage in range(5):
            s_advance(i + 1 - LAG[stage], stage)

    @pl.loop(CHUNKS, CHUNKS + LAG[4])
    def _(i):
        for stage in range(1, 5):
            s_advance(i - LAG[stage], stage)

    await_bytes(part.at[pl.ds(0, CHUNKS * (512 + 504))], ss_sem)
    await_bytes(wide.at[pl.ds(0, 32 * 127)], gs_sem)

    total = jnp.sum(final[0:8, :], keepdims=True) + PRIOR_WEIGHT
    out_ref[...] = (final[8:72, :] + PRIOR_WEIGHT * own_t[...].astype(F32)) / total


def body(images, precision, templates, template_id, shift_table):
    vmem = pl.BlockSpec(memory_space=pltpu.VMEM)
    anywhere = pl.BlockSpec(memory_space=pl.ANY)
    dma = pltpu.SemaphoreType.DMA
    img = images.reshape(N_IMG, 2, 32, 128).transpose(0, 2, 1, 3).reshape(N_IMG * ROWS, 128)
    own = templates.reshape(2, 32, 128).transpose(1, 0, 2).reshape(ROWS, 128)
    tab = jnp.asarray(phase_constant())
    out = pl.pallas_call(
        em_kernel,
        out_shape=jax.ShapeDtypeStruct((ROWS, 128), F32),
        in_specs=[anywhere, anywhere, vmem, vmem, vmem, vmem], out_specs=vmem,
        scratch_shapes=[
            pltpu.VMEM((N_IMG, 2 * COEFFS), BF16),
            pltpu.VMEM((2, 4096, 128), BF16),
            pltpu.VMEM((TEMPLATES * PITCH, 128), F32),
            pltpu.VMEM((PAIRS, COEFFS), F32),
            pltpu.VMEM((PAIRS, N_IMG), F32),
            pltpu.VMEM((PAIRS, STEP), BF16),
            pltpu.VMEM((PAIRS, STEP), BF16),
            pltpu.VMEM((PAIRS, STEP), F32),
            pltpu.VMEM((PAIRS, STEP), F32),
            pltpu.VMEM((2, PAIRS, N_IMG), BF16),
            pltpu.VMEM((PAIRS, 192), BF16),
            pltpu.VMEM((PAIRS, 128), F32),
            pltpu.VMEM((TEMPLATES, 128), F32),
            pltpu.VMEM((192, COEFFS), BF16),
            pltpu.VMEM((2, 4, 4, 4, ROWS, 128), BF16),
            pltpu.VMEM((CHUNKS * 1024, 128), F32),
            pltpu.VMEM((CHUNKS, 512, 128), F32),
            pltpu.VMEM((CHUNKS, 4, 4, 4, 8, 128), F32),
            pltpu.VMEM((CHUNKS, 3, 4, 4, 8, 128), F32),
            pltpu.VMEM((CHUNKS, 3, 4, 8, 128), F32),
            pltpu.VMEM((CHUNKS, 3, 8, 128), F32),
            pltpu.VMEM((72, 128), F32),
            dma((2,)), dma, dma, dma((4, 4)),
            dma, dma((CHUNKS, 4)),
        ],
        compiler_params=pltpu.CompilerParams(collective_id=0, has_side_effects=True,
                                             vmem_limit_bytes=60 * MIB),
        name="em_step",
    )(img, tab, own, precision.reshape(1, N_IMG), template_id.reshape(1, TEMPLATES), shift_table.T)
    return out.reshape(32, 2, 128).transpose(1, 0, 2).reshape(1, 2, COEFFS)


def solution(mesh):
    return jax.shard_map(
        body,
        mesh=mesh,
        in_specs=(
            P(("row", "col"), None, None),
            P(("row", "col")),
            P(("row", "col"), None, None),
            P(),
            P(),
        ),
        out_specs=P(("row", "col"), None, None),
        check_vma=False,
    )
```

```python
import functools

import jax
import jax.numpy as jnp
import ml_dtypes
import numpy as np
from jax import lax
from jax.experimental import pallas as pl
from jax.experimental.pallas import tpu as pltpu
from jax.sharding import PartitionSpec as P

MESH = pl.DeviceIdType.MESH
F32 = jnp.float32
BF16 = jnp.bfloat16

GRID = 64
COEFFS = 4096
TEMPLATES = 128
SHIFTS = 8
PAIRS = TEMPLATES * SHIFTS
N_IMG = 512
ROWS = 64
STEP = 512
STEPS = 2 * COEFFS // STEP
HALF_STEPS = STEPS // 2
PITCH = 65
LAG = (0, 2, 7, 15, 23)
CHUNKS = 9
PRIOR_WEIGHT = 4.0
RB, BB = 32, 16
MIB = 1 << 20

ORDERS = ((2, 1, 0), (1, 0, 2), (0, 2, 1))


def phase_constant():
    c = np.arange(COEFFS)
    fx = c // GRID - GRID // 2
    fy = c % GRID - GRID // 2
    s = np.arange(64)
    k = ((s // 8 - 4)[:, None] * fx[None] + (s % 8 - 4)[:, None] * fy[None]) % GRID
    angle = k * (2.0 * np.pi / GRID)
    both = np.stack([np.cos(angle), np.sin(angle)], 1).reshape(64, 2, 32, 128)
    both = both.transpose(0, 2, 1, 3).reshape(64, 2 * COEFFS)[:, :COEFFS].astype(np.float32)
    high = both.astype(ml_dtypes.bfloat16)
    rest = both - high.astype(np.float32)
    mid = rest.astype(ml_dtypes.bfloat16)
    low = (rest - mid.astype(np.float32)).astype(ml_dtypes.bfloat16)
    return np.concatenate([high, mid, low], 0)


def place():
    row, col = lax.axis_index("row"), lax.axis_index("col")
    z, y_lo = row % 4, row // 4
    core, x, y_hi = col % 2, (col // 2) % 4, col // 8
    return core, (z, y_hi * 2 + y_lo, x)


def device(core, at):
    z, y, x = at
    return ((y % 2) * 4 + z, ((y // 2) * 4 + x) * 2 + core)


def moved(at, axis, by):
    return tuple((v + by) % 4 if i == axis else v for i, v in enumerate(at))


def enter(core, at):
    barrier = pltpu.get_barrier_semaphore()
    others = [device(1 - core, at)]
    others += [device(core, moved(at, a, d)) for a in range(3) for d in (1, 2, 3)]
    for other in others:
        pl.semaphore_signal(barrier, inc=1, device_id=other, device_id_type=MESH)
    pl.semaphore_wait(barrier, len(others))


def em_kernel(img, tab, own_t, prec, tid, table, out_ref,
              x, raw, wide, fac, acc, rot_a, rot_b, buf_a, buf_b, wts, onehot, sign, norm, tabs,
              got, part, r0, mine, r1, r2, r3, final,
              img_sem, tab_sem, gs_sem, gr_sem, ss_sem, sr_sem):
    core, at = place()

    groups = [pl.ds(16 * g, 16) for g in range(4)]

    def view(rows, order, stage, where):
        done = order[:stage]
        index = tuple(slice(None) if a in done else where[a] for a in range(3))
        return got.at[(core,) + index + (rows,)]

    def g_copy(g, stage, d, order):
        rows = groups[g]
        if stage == 3:
            ref = got.at[core, :, :, :, rows]
            target = device(1 - core, at)
        else:
            ref = view(rows, order, stage, at)
            target = device(core, moved(at, order[stage], d))
        return pltpu.make_async_remote_copy(
            src_ref=ref, dst_ref=ref, send_sem=gs_sem, recv_sem=gr_sem.at[g, stage],
            device_id=target, device_id_type=MESH)

    def await_bytes(ref, sem):
        pltpu.make_async_copy(ref, ref, sem).wait()

    def g_each(stage):
        return (1, 3, 2) if stage < 3 else (1,)

    def g_stage(stage):
        for g in range(4):
            if stage:
                await_bytes(raw.at[0, pl.ds(0, 16 * (3, 12, 48, 64)[stage - 1])], gr_sem.at[g, stage - 1])
            if stage < 4 and g < 3:
                for d in g_each(stage):
                    g_copy(g, stage, d, ORDERS[g]).start()
            elif stage < 4:
                for o in (0, 2):
                    @pl.when(core * 2 == o)
                    def _():
                        for d in g_each(stage):
                            g_copy(g, stage, d, ORDERS[o]).start()

    lands = (r0, r1, r2, r3)

    def s_copy(c, o, stage, d):
        order = ORDERS[o]
        if stage == 0:
            src = part.at[pl.ds(pl.multiple_of(c * 1024 + (1 - core) * 512, 512), 512)]
            dst = r0.at[c]
            target = device(1 - core, at)
        else:
            axis = order[stage - 1]
            other = moved(at, axis, d)
            index = [at[a] if a in order[:stage - 1] else slice(None) for a in range(3)]
            index[axis] = other[axis]
            src = mine.at[(c,) + tuple(index)]
            dst = lands[stage].at[c, d - 1]
            target = device(core, other)
        return pltpu.make_async_remote_copy(
            src_ref=src, dst_ref=dst, send_sem=ss_sem,
            recv_sem=sr_sem.at[c, stage], device_id=target, device_id_type=MESH)

    def s_each(stage):
        return (1, 3, 2) if stage else (1,)

    def s_take(c, o, stage):
        await_bytes(lands[stage].at[c], sr_sem.at[c, stage])
        if stage == 0:
            total = part[pl.ds(pl.multiple_of(c * 1024 + core * 512, 512), 512), :] + r0[c]
            mine[c] = total.reshape(4, 4, 4, 8, 128)
            return
        index = (c,) + tuple(at[a] if a in ORDERS[o][:stage] else slice(None) for a in range(3))
        total = mine[index]
        for d in (1, 2, 3):
            total += lands[stage][c, d - 1]
        if stage == 3:
            final[pl.ds(pl.multiple_of(c * 8, 8), 8), :] = total
        else:
            mine[index] = total

    def s_advance(c, stage):
        @pl.when(jnp.logical_and(c >= 0, c < CHUNKS))
        def _():
            for o in range(3):
                @pl.when(c % 3 == o)
                def _():
                    if stage:
                        s_take(c, o, stage - 1)
                    if stage < 4:
                        for d in s_each(stage):
                            s_copy(c, o, stage, d).start()

    def fetch(b):
        return pltpu.make_async_copy(img.at[pl.ds(b * 4096, 4096)], raw.at[b % 2], img_sem.at[b % 2])

    def relayout(b):
        if b < 7:
            fetch(b + 1).start()
        fetch(b).wait()

        @pl.loop(0, 8)
        def _(i):
            for k in range(8):
                n = i * 8 + k
                rows = pl.ds(pl.multiple_of(n * ROWS, ROWS), ROWS)
                wide[pl.ds(n * PITCH, ROWS)] = raw[b % 2, rows].astype(F32)

        @pl.loop(0, ROWS // 8)
        def _(i):
            for k in range(8):
                r = i * 8 + k
                lanes = pl.ds(pl.multiple_of(r * 128, 128), 128)
                x[pl.ds(b * 64, 64), lanes] = wide[pl.ds(r, 64, stride=PITCH), :].astype(BF16)

    def choose():
        ids = lax.broadcasted_iota(jnp.int32, (128, 128), 0)
        pick = jnp.where(ids == tid[...], 1.0, 0.0).astype(BF16)
        shifts_t = jnp.dot(table[...].astype(F32).astype(BF16), pick, preferred_element_type=F32)
        slot = lax.broadcasted_iota(jnp.int32, (128, 128), 1)
        row, col = slot // 16, slot % 16
        inner = (col % 2) * 64 + (row % 4) * 16 + ((col // 8) * 2 + row // 4) * 4 + (col // 2) % 4
        perm = jnp.where(ids == inner, 1.0, 0.0).astype(BF16)
        shifts = lax.dot_general(perm, shifts_t.astype(BF16), (((1,), (1,)), ((), ())),
                                 preferred_element_type=F32)
        lane = lax.broadcasted_iota(jnp.int32, (128, 64), 1).astype(F32)
        odd_lane = jnp.where((lax.broadcasted_iota(jnp.int32, (128, 64), 1) // 8) % 2 == 1, 1.0, 0.0)
        for j in range(SHIFTS):
            one = jnp.where(lane == shifts[:, j:j + 1], 1.0, 0.0)
            odd = jnp.sum(one * odd_lane, axis=1, keepdims=True)
            sign[pl.ds(j * 128, 128), :] = jnp.broadcast_to(1.0 - 2.0 * odd, (128, 128))
            one = one.astype(BF16)
            onehot[pl.ds(j * 128, 128), :] = jnp.concatenate([one, one, one], axis=1)

    def widen(half):
        @pl.loop(0, 16)
        def _(i):
            for k in range(4):
                rows = pl.ds((half * 64 + i * 4 + k) * PITCH, ROWS)
                wide[rows] = got[half, i // 4, i % 4, k].astype(F32)

    tab_copy = pltpu.make_async_copy(tab, tabs, tab_sem)
    fetch(0).start()
    tab_copy.start()
    enter(core, at)
    got[core, at[0], at[1], at[2]] = own_t[...]
    g_stage(0)
    choose()
    norm[...] = jnp.zeros_like(norm)
    acc[...] = jnp.zeros_like(acc)
    relayout(0)
    relayout(1)
    g_stage(1)
    for b in (2, 3, 4):
        relayout(b)
    g_stage(2)
    for b in (5, 6, 7):
        relayout(b)
    g_stage(3)
    widen(core)
    tab_copy.wait()
    for k in range(4):
        lanes = slice(k * 1024, k * 1024 + 1024)
        fac[:, lanes] = jnp.dot(onehot[...], tabs[:, lanes], preferred_element_type=F32)
    g_stage(4)
    widen(1 - core)

    def factor(q, rows, tile):
        start = pl.multiple_of((q % HALF_STEPS) * STEP + tile * 256, 256)
        return fac[rows, pl.ds(start, 128)], fac[rows, pl.ds(start + 128, 128)]

    def rotate(q, rot):
        count = jnp.where(q < STEPS, 1.0, 0.0)
        for b in range(TEMPLATES // RB):
            squares = jnp.zeros((RB, 128), F32)
            for tile in range(2):
                r = b * RB * PITCH + ((q + HALF_STEPS) % STEPS) * 4 + 2 * tile
                re = wide[pl.ds(r, RB, stride=PITCH), :]
                im = wide[pl.ds(r + 1, RB, stride=PITCH), :]
                squares += re * re + im * im
                for j in range(SHIFTS):
                    rows = pl.ds(j * 128 + b * RB, RB)
                    c, s = factor(q, rows, tile)
                    rot[rows, tile * 256:tile * 256 + 128] = (re * c + im * s).astype(BF16)
                    rot[rows, tile * 256 + 128:tile * 256 + 256] = (im * c - re * s).astype(BF16)
            norm[b * RB:b * RB + RB, :] += squares * count

    def images(q):
        return x[:, pl.ds(pl.multiple_of((q % STEPS) * STEP, STEP), STEP)]

    def add_scores(q, rot):
        acc[...] += lax.dot_general(rot[...], images(q + HALF_STEPS), (((1,), (1,)), ((), ())),
                                    preferred_element_type=F32)

    def four(value):
        return jnp.concatenate([value] * 4, axis=1)

    rotate(0, rot_a)

    @pl.loop(0, 2)
    def _(half):
        @pl.loop(0, PAIRS // 32)
        def _(i):
            rows = pl.ds(pl.multiple_of(i * 32, 32), 32)
            acc[rows, :] *= four(sign[rows, :])

        @pl.loop(0, HALF_STEPS // 2)
        def _(i):
            q = half * HALF_STEPS + 2 * i
            add_scores(q, rot_a)
            rotate(q + 1, rot_b)
            add_scores(q + 1, rot_b)
            rotate(q + 2, rot_a)

    precision = prec[...]
    norm[...] = jnp.broadcast_to(0.5 * jnp.sum(norm[...], axis=1, keepdims=True), (TEMPLATES, 128))

    def score(i, top):
        rows = pl.ds(pl.multiple_of(i * 8, 8), 8)
        half = norm[pl.ds(pl.multiple_of((i % 16) * 8, 8), 8), :]
        value = precision * (acc[rows, :] - four(half))
        acc[rows, :] = value
        return jnp.maximum(top, value)

    top = lax.fori_loop(0, PAIRS // 8, score, jnp.full((8, N_IMG), -jnp.inf, F32), unroll=4)
    top = jnp.max(top, axis=0, keepdims=True)

    def exponent(i, total):
        rows = pl.ds(pl.multiple_of(i * 8, 8), 8)
        value = jnp.exp(acc[rows, :] - top)
        acc[rows, :] = value
        return total + value

    total = lax.fori_loop(0, PAIRS // 8, exponent, jnp.zeros((8, N_IMG), F32), unroll=4)
    scale = 1.0 / jnp.sum(total, axis=0, keepdims=True)

    @pl.loop(0, TEMPLATES // 16)
    def _(b):
        total = jnp.zeros((16, 128), F32)
        for j in range(SHIFTS):
            rows = pl.ds(pl.multiple_of(j * 128 + b * 16, 16), 16)
            weight = (acc[rows, :] * scale).astype(BF16)
            wts[0, rows, :] = weight
            weight = weight.astype(F32)
            wts[1, rows, :] = (weight * four(sign[rows, :])).astype(BF16)
            for lanes in range(4):
                total += weight[:, lanes * 128:lanes * 128 + 128]
        part[pl.ds(b * 128, 16, stride=8), :] = total
        for r in range(1, 8):
            part[pl.ds(b * 128 + r, 16, stride=8), :] = jnp.zeros((16, 128), F32)

    s_advance(jnp.int32(0), 0)

    def gather_images(q, buf):
        buf[...] = jnp.dot(wts[(q // HALF_STEPS) % 2], images(q), preferred_element_type=F32)

    def turn_back(q, buf, chunk, odd):
        for b in range(TEMPLATES // BB):
            for tile in range(2):
                back_re = jnp.zeros((BB, 128), F32)
                back_im = jnp.zeros((BB, 128), F32)
                for j in range(SHIFTS):
                    rows = pl.ds(j * 128 + b * BB, BB)
                    c, s = factor(q, rows, tile)
                    re = buf[rows, tile * 256:tile * 256 + 128]
                    im = buf[rows, tile * 256 + 128:tile * 256 + 256]
                    back_re += re * c - im * s
                    back_im += im * c + re * s
                r = chunk * 1024 + b * BB * 8 + odd * 4 + 2 * tile
                part[pl.ds(r, BB, stride=8), :] = back_re
                part[pl.ds(r + 1, BB, stride=8), :] = back_im

    gather_images(jnp.int32(0), buf_a)

    @pl.loop(0, STEPS // 2)
    def _(i):
        gather_images(2 * i + 1, buf_b)
        turn_back(2 * i, buf_a, i + 1, 0)
        gather_images(2 * i + 2, buf_a)
        turn_back(2 * i + 1, buf_b, i + 1, 1)
        for stage in range(5):
            s_advance(i + 1 - LAG[stage], stage)

    @pl.loop(CHUNKS, CHUNKS + LAG[4])
    def _(i):
        for stage in range(1, 5):
            s_advance(i - LAG[stage], stage)

    await_bytes(part.at[pl.ds(0, CHUNKS * (512 + 504))], ss_sem)
    await_bytes(wide.at[pl.ds(0, 32 * 127)], gs_sem)

    total = jnp.sum(final[0:8, :], keepdims=True) + PRIOR_WEIGHT
    out_ref[...] = (final[8:72, :] + PRIOR_WEIGHT * own_t[...].astype(F32)) / total


def body(images, precision, templates, template_id, shift_table):
    vmem = pl.BlockSpec(memory_space=pltpu.VMEM)
    anywhere = pl.BlockSpec(memory_space=pl.ANY)
    dma = pltpu.SemaphoreType.DMA
    img = images.reshape(N_IMG, 2, 32, 128).transpose(0, 2, 1, 3).reshape(N_IMG * ROWS, 128)
    own = templates.reshape(2, 32, 128).transpose(1, 0, 2).reshape(ROWS, 128)
    tab = jnp.asarray(phase_constant())
    out = pl.pallas_call(
        em_kernel,
        out_shape=jax.ShapeDtypeStruct((ROWS, 128), F32),
        in_specs=[anywhere, anywhere, vmem, vmem, vmem, vmem], out_specs=vmem,
        scratch_shapes=[
            pltpu.VMEM((N_IMG, 2 * COEFFS), BF16),
            pltpu.VMEM((2, 4096, 128), BF16),
            pltpu.VMEM((TEMPLATES * PITCH, 128), F32),
            pltpu.VMEM((PAIRS, COEFFS), F32),
            pltpu.VMEM((PAIRS, N_IMG), F32),
            pltpu.VMEM((PAIRS, STEP), BF16),
            pltpu.VMEM((PAIRS, STEP), BF16),
            pltpu.VMEM((PAIRS, STEP), F32),
            pltpu.VMEM((PAIRS, STEP), F32),
            pltpu.VMEM((2, PAIRS, N_IMG), BF16),
            pltpu.VMEM((PAIRS, 192), BF16),
            pltpu.VMEM((PAIRS, 128), F32),
            pltpu.VMEM((TEMPLATES, 128), F32),
            pltpu.VMEM((192, COEFFS), BF16),
            pltpu.VMEM((2, 4, 4, 4, ROWS, 128), BF16),
            pltpu.VMEM((CHUNKS * 1024, 128), F32),
            pltpu.VMEM((CHUNKS, 512, 128), F32),
            pltpu.VMEM((CHUNKS, 4, 4, 4, 8, 128), F32),
            pltpu.VMEM((CHUNKS, 3, 4, 4, 8, 128), F32),
            pltpu.VMEM((CHUNKS, 3, 4, 8, 128), F32),
            pltpu.VMEM((CHUNKS, 3, 8, 128), F32),
            pltpu.VMEM((72, 128), F32),
            dma((2,)), dma, dma, dma((4, 4)),
            dma, dma((CHUNKS, 4)),
        ],
        compiler_params=pltpu.CompilerParams(collective_id=0, has_side_effects=True,
                                             vmem_limit_bytes=60 * MIB),
        name="em_step",
    )(img, tab, own, precision.reshape(1, N_IMG), template_id.reshape(1, TEMPLATES), shift_table.T)
    return out.reshape(32, 2, 128).transpose(1, 0, 2).reshape(1, 2, COEFFS)


def solution(mesh):
    return jax.shard_map(
        body,
        mesh=mesh,
        in_specs=(
            P(("row", "col"), None, None),
            P(("row", "col")),
            P(("row", "col"), None, None),
            P(),
            P(),
        ),
        out_specs=P(("row", "col"), None, None),
        check_vma=False,
    )
```

```python
import functools

import jax
import jax.numpy as jnp
import ml_dtypes
import numpy as np
from jax import lax
from jax.experimental import pallas as pl
from jax.experimental.pallas import tpu as pltpu
from jax.sharding import PartitionSpec as P

MESH = pl.DeviceIdType.MESH
F32 = jnp.float32
BF16 = jnp.bfloat16

GRID = 64
COEFFS = 4096
TEMPLATES = 128
SHIFTS = 8
PAIRS = TEMPLATES * SHIFTS
N_IMG = 512
ROWS = 64
STEP = 512
STEPS = 2 * COEFFS // STEP
HALF_STEPS = STEPS // 2
PITCH = 65
LAG = (0, 2, 7, 15, 23)
CHUNKS = 9
PRIOR_WEIGHT = 4.0
RB, BB = 32, 16
MIB = 1 << 20

ORDERS = ((2, 1, 0), (1, 0, 2), (0, 2, 1))


def phase_constant():
    c = np.arange(COEFFS)
    fx = c // GRID - GRID // 2
    fy = c % GRID - GRID // 2
    s = np.arange(64)
    k = ((s // 8 - 4)[:, None] * fx[None] + (s % 8 - 4)[:, None] * fy[None]) % GRID
    angle = k * (2.0 * np.pi / GRID)
    both = np.stack([np.cos(angle), np.sin(angle)], 1).reshape(64, 2, 32, 128)
    both = both.transpose(0, 2, 1, 3).reshape(64, 2 * COEFFS)[:, :COEFFS].astype(np.float32)
    high = both.astype(ml_dtypes.bfloat16)
    rest = both - high.astype(np.float32)
    mid = rest.astype(ml_dtypes.bfloat16)
    low = (rest - mid.astype(np.float32)).astype(ml_dtypes.bfloat16)
    return np.concatenate([high, mid, low], 0)


def place():
    row, col = lax.axis_index("row"), lax.axis_index("col")
    z, y_lo = row % 4, row // 4
    core, x, y_hi = col % 2, (col // 2) % 4, col // 8
    return core, (z, y_hi * 2 + y_lo, x)


def device(core, at):
    z, y, x = at
    return ((y % 2) * 4 + z, ((y // 2) * 4 + x) * 2 + core)


def moved(at, axis, by):
    return tuple((v + by) % 4 if i == axis else v for i, v in enumerate(at))


def enter(core, at):
    barrier = pltpu.get_barrier_semaphore()
    others = [device(1 - core, at)]
    others += [device(core, moved(at, a, d)) for a in range(3) for d in (1, 2, 3)]
    for other in others:
        pl.semaphore_signal(barrier, inc=1, device_id=other, device_id_type=MESH)
    pl.semaphore_wait(barrier, len(others))


def em_kernel(img, tab, own_t, prec, tid, table, out_ref,
              x, raw, wide, fac, acc, rot_a, rot_b, buf_a, buf_b, wts, onehot, sign, norm, tabs,
              got, part, r0, mine, r1, r2, r3, final,
              img_sem, tab_sem, gs_sem, gr_sem, ss_sem, sr_sem):
    core, at = place()

    groups = [pl.ds(16 * g, 16) for g in range(4)]

    def view(rows, order, stage, where):
        done = order[:stage]
        index = tuple(slice(None) if a in done else where[a] for a in range(3))
        return got.at[(core,) + index + (rows,)]

    def g_copy(g, stage, d, order):
        rows = groups[g]
        if stage == 3:
            ref = got.at[core, :, :, :, rows]
            target = device(1 - core, at)
        else:
            ref = view(rows, order, stage, at)
            target = device(core, moved(at, order[stage], d))
        return pltpu.make_async_remote_copy(
            src_ref=ref, dst_ref=ref, send_sem=gs_sem, recv_sem=gr_sem.at[g, stage],
            device_id=target, device_id_type=MESH)

    def await_bytes(ref, sem):
        pltpu.make_async_copy(ref, ref, sem).wait()

    def g_each(stage):
        return (1, 3, 2) if stage < 3 else (1,)

    def g_stage(stage):
        for g in range(4):
            if stage:
                await_bytes(raw.at[0, pl.ds(0, 16 * (3, 12, 48, 64)[stage - 1])], gr_sem.at[g, stage - 1])
            if stage < 4 and g < 3:
                for d in g_each(stage):
                    g_copy(g, stage, d, ORDERS[g]).start()
            elif stage < 4:
                for o in (0, 2):
                    @pl.when(core * 2 == o)
                    def _():
                        for d in g_each(stage):
                            g_copy(g, stage, d, ORDERS[o]).start()

    lands = (r0, r1, r2, r3)

    def s_copy(c, o, stage, d):
        order = ORDERS[o]
        if stage == 0:
            src = part.at[pl.ds(pl.multiple_of(c * 1024 + (1 - core) * 512, 512), 512)]
            dst = r0.at[c]
            target = device(1 - core, at)
        else:
            axis = order[stage - 1]
            other = moved(at, axis, d)
            index = [at[a] if a in order[:stage - 1] else slice(None) for a in range(3)]
            index[axis] = other[axis]
            src = mine.at[(c,) + tuple(index)]
            dst = lands[stage].at[c, d - 1]
            target = device(core, other)
        return pltpu.make_async_remote_copy(
            src_ref=src, dst_ref=dst, send_sem=ss_sem,
            recv_sem=sr_sem.at[c, stage], device_id=target, device_id_type=MESH)

    def s_each(stage):
        return (1, 3, 2) if stage else (1,)

    def s_take(c, o, stage):
        await_bytes(lands[stage].at[c], sr_sem.at[c, stage])
        if stage == 0:
            total = part[pl.ds(pl.multiple_of(c * 1024 + core * 512, 512), 512), :] + r0[c]
            mine[c] = total.reshape(4, 4, 4, 8, 128)
            return
        index = (c,) + tuple(at[a] if a in ORDERS[o][:stage] else slice(None) for a in range(3))
        total = mine[index]
        for d in (1, 2, 3):
            total += lands[stage][c, d - 1]
        if stage == 3:
            final[pl.ds(pl.multiple_of(c * 8, 8), 8), :] = total
        else:
            mine[index] = total

    def s_advance(c, stage):
        @pl.when(jnp.logical_and(c >= 0, c < CHUNKS))
        def _():
            for o in range(3):
                @pl.when(c % 3 == o)
                def _():
                    if stage:
                        s_take(c, o, stage - 1)
                    if stage < 4:
                        for d in s_each(stage):
                            s_copy(c, o, stage, d).start()

    def fetch(b):
        return pltpu.make_async_copy(img.at[pl.ds(b * 4096, 4096)], raw.at[b % 2], img_sem.at[b % 2])

    def relayout(b):
        if b < 7:
            fetch(b + 1).start()
        fetch(b).wait()

        @pl.loop(0, 8)
        def _(i):
            for k in range(8):
                n = i * 8 + k
                rows = pl.ds(pl.multiple_of(n * ROWS, ROWS), ROWS)
                wide[pl.ds(n * PITCH, ROWS)] = raw[b % 2, rows].astype(F32)

        @pl.loop(0, ROWS // 8)
        def _(i):
            for k in range(8):
                r = i * 8 + k
                lanes = pl.ds(pl.multiple_of(r * 128, 128), 128)
                x[pl.ds(b * 64, 64), lanes] = wide[pl.ds(r, 64, stride=PITCH), :].astype(BF16)

    def choose():
        ids = lax.broadcasted_iota(jnp.int32, (128, 128), 0)
        pick = jnp.where(ids == tid[...], 1.0, 0.0).astype(BF16)
        shifts_t = jnp.dot(table[...].astype(F32).astype(BF16), pick, preferred_element_type=F32)
        slot = lax.broadcasted_iota(jnp.int32, (128, 128), 1)
        row, col = slot // 16, slot % 16
        inner = (col % 2) * 64 + (row % 4) * 16 + ((col // 8) * 2 + row // 4) * 4 + (col // 2) % 4
        perm = jnp.where(ids == inner, 1.0, 0.0).astype(BF16)
        shifts = lax.dot_general(perm, shifts_t.astype(BF16), (((1,), (1,)), ((), ())),
                                 preferred_element_type=F32)
        lane = lax.broadcasted_iota(jnp.int32, (128, 64), 1).astype(F32)
        odd_lane = jnp.where((lax.broadcasted_iota(jnp.int32, (128, 64), 1) // 8) % 2 == 1, 1.0, 0.0)
        for j in range(SHIFTS):
            one = jnp.where(lane == shifts[:, j:j + 1], 1.0, 0.0)
            odd = jnp.sum(one * odd_lane, axis=1, keepdims=True)
            sign[pl.ds(j * 128, 128), :] = jnp.broadcast_to(1.0 - 2.0 * odd, (128, 128))
            one = one.astype(BF16)
            onehot[pl.ds(j * 128, 128), :] = jnp.concatenate([one, one, one], axis=1)

    def widen(half):
        @pl.loop(0, 16)
        def _(i):
            for k in range(4):
                rows = pl.ds((half * 64 + i * 4 + k) * PITCH, ROWS)
                wide[rows] = got[half, i // 4, i % 4, k].astype(F32)

    tab_copy = pltpu.make_async_copy(tab, tabs, tab_sem)
    fetch(0).start()
    tab_copy.start()
    enter(core, at)
    got[core, at[0], at[1], at[2]] = own_t[...]
    g_stage(0)
    choose()
    norm[...] = jnp.zeros_like(norm)
    acc[...] = jnp.zeros_like(acc)
    relayout(0)
    g_stage(1)
    relayout(1)
    relayout(2)
    g_stage(2)
    for b in range(3, 8):
        relayout(b)
    g_stage(3)
    widen(core)
    tab_copy.wait()
    for k in range(4):
        lanes = slice(k * 1024, k * 1024 + 1024)
        fac[:, lanes] = jnp.dot(onehot[...], tabs[:, lanes], preferred_element_type=F32)
    g_stage(4)
    widen(1 - core)

    def factor(q, rows, tile):
        start = pl.multiple_of((q % HALF_STEPS) * STEP + tile * 256, 256)
        return fac[rows, pl.ds(start, 128)], fac[rows, pl.ds(start + 128, 128)]

    def rotate(q, rot):
        count = jnp.where(q < STEPS, 1.0, 0.0)
        for b in range(TEMPLATES // RB):
            squares = jnp.zeros((RB, 128), F32)
            for tile in range(2):
                r = b * RB * PITCH + ((q + HALF_STEPS) % STEPS) * 4 + 2 * tile
                re = wide[pl.ds(r, RB, stride=PITCH), :]
                im = wide[pl.ds(r + 1, RB, stride=PITCH), :]
                squares += re * re + im * im
                for j in range(SHIFTS):
                    rows = pl.ds(j * 128 + b * RB, RB)
                    c, s = factor(q, rows, tile)
                    rot[rows, tile * 256:tile * 256 + 128] = (re * c + im * s).astype(BF16)
                    rot[rows, tile * 256 + 128:tile * 256 + 256] = (im * c - re * s).astype(BF16)
            norm[b * RB:b * RB + RB, :] += squares * count

    def images(q):
        return x[:, pl.ds(pl.multiple_of((q % STEPS) * STEP, STEP), STEP)]

    def add_scores(q, rot):
        acc[...] += lax.dot_general(rot[...], images(q + HALF_STEPS), (((1,), (1,)), ((), ())),
                                    preferred_element_type=F32)

    def four(value):
        return jnp.concatenate([value] * 4, axis=1)

    rotate(0, rot_a)

    @pl.loop(0, 2)
    def _(half):
        @pl.loop(0, PAIRS // 32)
        def _(i):
            rows = pl.ds(pl.multiple_of(i * 32, 32), 32)
            acc[rows, :] *= four(sign[rows, :])

        @pl.loop(0, HALF_STEPS // 2)
        def _(i):
            q = half * HALF_STEPS + 2 * i
            add_scores(q, rot_a)
            rotate(q + 1, rot_b)
            add_scores(q + 1, rot_b)
            rotate(q + 2, rot_a)

    precision = prec[...]
    norm[...] = jnp.broadcast_to(0.5 * jnp.sum(norm[...], axis=1, keepdims=True), (TEMPLATES, 128))

    def score(i, top):
        rows = pl.ds(pl.multiple_of(i * 8, 8), 8)
        half = norm[pl.ds(pl.multiple_of((i % 16) * 8, 8), 8), :]
        value = precision * (acc[rows, :] - four(half))
        acc[rows, :] = value
        return jnp.maximum(top, value)

    top = lax.fori_loop(0, PAIRS // 8, score, jnp.full((8, N_IMG), -jnp.inf, F32), unroll=4)
    top = jnp.max(top, axis=0, keepdims=True)

    def exponent(i, total):
        rows = pl.ds(pl.multiple_of(i * 8, 8), 8)
        value = jnp.exp(acc[rows, :] - top)
        acc[rows, :] = value
        return total + value

    total = lax.fori_loop(0, PAIRS // 8, exponent, jnp.zeros((8, N_IMG), F32), unroll=4)
    scale = 1.0 / jnp.sum(total, axis=0, keepdims=True)

    @pl.loop(0, TEMPLATES // 16)
    def _(b):
        total = jnp.zeros((16, 128), F32)
        for j in range(SHIFTS):
            rows = pl.ds(pl.multiple_of(j * 128 + b * 16, 16), 16)
            weight = (acc[rows, :] * scale).astype(BF16)
            wts[0, rows, :] = weight
            weight = weight.astype(F32)
            wts[1, rows, :] = (weight * four(sign[rows, :])).astype(BF16)
            for lanes in range(4):
                total += weight[:, lanes * 128:lanes * 128 + 128]
        part[pl.ds(b * 128, 16, stride=8), :] = total
        for r in range(1, 8):
            part[pl.ds(b * 128 + r, 16, stride=8), :] = jnp.zeros((16, 128), F32)

    s_advance(jnp.int32(0), 0)

    def gather_images(q, buf):
        buf[...] = jnp.dot(wts[(q // HALF_STEPS) % 2], images(q), preferred_element_type=F32)

    def turn_back(q, buf, chunk, odd):
        for b in range(TEMPLATES // BB):
            for tile in range(2):
                back_re = jnp.zeros((BB, 128), F32)
                back_im = jnp.zeros((BB, 128), F32)
                for j in range(SHIFTS):
                    rows = pl.ds(j * 128 + b * BB, BB)
                    c, s = factor(q, rows, tile)
                    re = buf[rows, tile * 256:tile * 256 + 128]
                    im = buf[rows, tile * 256 + 128:tile * 256 + 256]
                    back_re += re * c - im * s
                    back_im += im * c + re * s
                r = chunk * 1024 + b * BB * 8 + odd * 4 + 2 * tile
                part[pl.ds(r, BB, stride=8), :] = back_re
                part[pl.ds(r + 1, BB, stride=8), :] = back_im

    gather_images(jnp.int32(0), buf_a)

    @pl.loop(0, STEPS // 2)
    def _(i):
        gather_images(2 * i + 1, buf_b)
        turn_back(2 * i, buf_a, i + 1, 0)
        gather_images(2 * i + 2, buf_a)
        turn_back(2 * i + 1, buf_b, i + 1, 1)
        for stage in range(5):
            s_advance(i + 1 - LAG[stage], stage)

    @pl.loop(CHUNKS, CHUNKS + LAG[4])
    def _(i):
        for stage in range(1, 5):
            s_advance(i - LAG[stage], stage)

    await_bytes(part.at[pl.ds(0, CHUNKS * (512 + 504))], ss_sem)
    await_bytes(wide.at[pl.ds(0, 32 * 127)], gs_sem)

    total = jnp.sum(final[0:8, :], keepdims=True) + PRIOR_WEIGHT
    out_ref[...] = (final[8:72, :] + PRIOR_WEIGHT * own_t[...].astype(F32)) / total


def body(images, precision, templates, template_id, shift_table):
    vmem = pl.BlockSpec(memory_space=pltpu.VMEM)
    anywhere = pl.BlockSpec(memory_space=pl.ANY)
    dma = pltpu.SemaphoreType.DMA
    img = images.reshape(N_IMG, 2, 32, 128).transpose(0, 2, 1, 3).reshape(N_IMG * ROWS, 128)
    own = templates.reshape(2, 32, 128).transpose(1, 0, 2).reshape(ROWS, 128)
    tab = jnp.asarray(phase_constant())
    out = pl.pallas_call(
        em_kernel,
        out_shape=jax.ShapeDtypeStruct((ROWS, 128), F32),
        in_specs=[anywhere, anywhere, vmem, vmem, vmem, vmem], out_specs=vmem,
        scratch_shapes=[
            pltpu.VMEM((N_IMG, 2 * COEFFS), BF16),
            pltpu.VMEM((2, 4096, 128), BF16),
            pltpu.VMEM((TEMPLATES * PITCH, 128), F32),
            pltpu.VMEM((PAIRS, COEFFS), F32),
            pltpu.VMEM((PAIRS, N_IMG), F32),
            pltpu.VMEM((PAIRS, STEP), BF16),
            pltpu.VMEM((PAIRS, STEP), BF16),
            pltpu.VMEM((PAIRS, STEP), F32),
            pltpu.VMEM((PAIRS, STEP), F32),
            pltpu.VMEM((2, PAIRS, N_IMG), BF16),
            pltpu.VMEM((PAIRS, 192), BF16),
            pltpu.VMEM((PAIRS, 128), F32),
            pltpu.VMEM((TEMPLATES, 128), F32),
            pltpu.VMEM((192, COEFFS), BF16),
            pltpu.VMEM((2, 4, 4, 4, ROWS, 128), BF16),
            pltpu.VMEM((CHUNKS * 1024, 128), F32),
            pltpu.VMEM((CHUNKS, 512, 128), F32),
            pltpu.VMEM((CHUNKS, 4, 4, 4, 8, 128), F32),
            pltpu.VMEM((CHUNKS, 3, 4, 4, 8, 128), F32),
            pltpu.VMEM((CHUNKS, 3, 4, 8, 128), F32),
            pltpu.VMEM((CHUNKS, 3, 8, 128), F32),
            pltpu.VMEM((72, 128), F32),
            dma((2,)), dma, dma, dma((4, 4)),
            dma, dma((CHUNKS, 4)),
        ],
        compiler_params=pltpu.CompilerParams(collective_id=0, has_side_effects=True,
                                             vmem_limit_bytes=60 * MIB),
        name="em_step",
    )(img, tab, own, precision.reshape(1, N_IMG), template_id.reshape(1, TEMPLATES), shift_table.T)
    return out.reshape(32, 2, 128).transpose(1, 0, 2).reshape(1, 2, COEFFS)


def solution(mesh):
    return jax.shard_map(
        body,
        mesh=mesh,
        in_specs=(
            P(("row", "col"), None, None),
            P(("row", "col")),
            P(("row", "col"), None, None),
            P(),
            P(),
        ),
        out_specs=P(("row", "col"), None, None),
        check_vma=False,
    )
```
